32 devices in a mesh: slab: 8 (over z, x), leaf: 4 (over y, core).
Axes of the slice: x: 2, y: 2, z: 4, core: 2. Of those that a mesh axis runs over, the one named last changes fastest.
Arguments:
- particles: float32 [3, 32, 16, 256], P(None, 'slab', 'leaf'), may hold values from -1.05 to 1.05, as said below
- near_mask: int32 [16, 32, 16], P(None, 'slab', 'leaf'), may hold values from 0 to 1, as said below
Outputs:
- velocity: float32 [2, 32, 16, 256], P(None, 'slab', 'leaf')
The draws below stay inside these ranges and needn't reach their ends.
Inputs may be any that keep to these rules, and one draw needn't show every extreme that they name: `particles`: entries 0 and 1 of the first dimension are offsets; entry 2 is the circulation. near_mask[o, i, j] = near_mask[15 - o, i + dx, j + dy], where (dx, dy) is step o of the 16 steps with max(|dx|, |dy|) = 2 in row-major order over dx, then dy; it is 0 where leaf (i + dx, j + dy) lies outside the grid.
All inputs are finite; a program needn't handle non-finite values.
Results may differ from the reference program's by a relative error of at most 0.0003.
Values sent between devices are 32-bit elements; how exact they have to be, the bound alone decides.
A program may use at most 64 MiB of HBM per device.

```python
import math
from functools import partial
import jax
import jax.numpy as jnp
import numpy as np
from jax import lax

C = 4
P_SIZE = 256
ORDER = 10
GX = 32
GY = 16
N_SLAB = 8
N_LEAF = 4


cycle_steps = [(a, b) for a in range(-2, 3) for b in range(-2, 3) if max(abs(a), abs(b)) == 2]


def leaf_classes(key):
    base_key = jax.random.fold_in(key, 7)
    first_key, second_key = jax.random.split(base_key)
    own_class = jax.random.randint(first_key, (GX, GY), 0, 2)
    region = jax.random.randint(second_key, (GX // 4, GY // 4), 0, 3)
    spread = jnp.repeat(jnp.repeat(region, 4, axis=0), 4, axis=1)
    return (own_class + spread).astype(jnp.int32)


def draw_particles(key, part):
    classes = leaf_classes(key)
    half_width = 0.3 + 0.25 * classes.astype(jnp.float32)
    draw_key = jax.random.fold_in(key, 11)
    key_x, key_y, key_strength = jax.random.split(draw_key, 3)
    offset_x = jax.random.uniform(key_x, (GX, GY, P_SIZE), jnp.float32, -1.0, 1.0) * half_width[:, :, None]
    offset_y = jax.random.uniform(key_y, (GX, GY, P_SIZE), jnp.float32, -1.0, 1.0) * half_width[:, :, None]
    strength = jax.random.normal(key_strength, (GX, GY, P_SIZE), jnp.float32) / 16.0
    return jnp.stack([offset_x, offset_y, strength])


def draw_near_mask(key, part):
    classes = leaf_classes(key)
    padded = jnp.pad(classes, 2, constant_values=-10)
    layers = []
    for step_x, step_y in cycle_steps:
        beside = padded[2 + step_x:2 + step_x + GX, 2 + step_y:2 + step_y + GY]
        layers.append((classes + beside >= 3).astype(jnp.int32))
    return jnp.stack(layers)


def setup_inputs(seed: int = 0) -> dict:
    keys = jax.random.split(jax.random.key(seed), 3)
    return {
        "particles": draw_particles(jax.random.fold_in(keys[2], 71), 0),
        "near_mask": draw_near_mask(jax.random.fold_in(keys[2], 71), 0),
    }


DELTA_SQUARED = 0.0025
TWO_PI = 2.0 * math.pi
inner_steps = [(a, b) for a in range(-1, 2) for b in range(-1, 2)]
cycle_steps = [(a, b) for a in range(-2, 3) for b in range(-2, 3) if max(abs(a), abs(b)) == 2]


def complex_powers(base_real, base_imaginary, count):
    power_real = [jnp.ones_like(base_real)]
    power_imaginary = [jnp.zeros_like(base_imaginary)]
    for repeat in range(1, count):
        last_real = power_real[-1]
        last_imaginary = power_imaginary[-1]
        power_real.append(last_real * base_real - last_imaginary * base_imaginary)
        power_imaginary.append(last_real * base_imaginary + last_imaginary * base_real)
    return jnp.stack(power_real, -1), jnp.stack(power_imaginary, -1)


def translation(shift_real, shift_imaginary):
    hankel = np.arange(ORDER)[:, None] + np.arange(ORDER)[None, :] + 1
    weights = np.array([[math.comb(i + k, k) * (-1.0) ** (k + 1) for k in range(ORDER)] for i in range(ORDER)], dtype=np.float32)
    denominator = shift_real * shift_real + shift_imaginary * shift_imaginary
    inverse_real = shift_real / denominator
    inverse_imaginary = -shift_imaginary / denominator
    power_real, power_imaginary = complex_powers(inverse_real, inverse_imaginary, 2 * ORDER)
    return power_real[..., hankel] * weights, power_imaginary[..., hankel] * weights


def apply_translation(matrix_real, matrix_imaginary, source_real, source_imaginary):
    source_real = source_real[..., None, :]
    source_imaginary = source_imaginary[..., None, :]
    out_real = jnp.sum(matrix_real * source_real - matrix_imaginary * source_imaginary, -1)
    out_imaginary = jnp.sum(matrix_real * source_imaginary + matrix_imaginary * source_real, -1)
    return out_real, out_imaginary


def pair_row(step_x, step_y, pieces):
    target_x, target_y, source_x, source_y, circulation = pieces
    delta_x = target_x[:, :, None] - (step_x + source_x[:, None, :])
    delta_y = target_y[:, :, None] - (step_y + source_y[:, None, :])
    factor = circulation[:, None, :] / (delta_x * delta_x + delta_y * delta_y + DELTA_SQUARED)
    return jnp.sum(factor * delta_x, -1), -jnp.sum(factor * delta_y, -1)


def reference(particles, near_mask):
    float_type = particles.dtype
    offset_x, offset_y, strength = particles[0], particles[1], particles[2]
    power_real, power_imaginary = complex_powers(offset_x, offset_y, ORDER)
    leaf_real = jnp.sum(strength[..., None] * power_real, axis=2)
    leaf_imaginary = jnp.sum(strength[..., None] * power_imaginary, axis=2)
    row_index = jnp.arange(GX, dtype=jnp.int32)
    column_index = jnp.arange(GY, dtype=jnp.int32)
    row_block = row_index // C
    column_block = column_index // C
    centred_x = (row_index % C).astype(float_type) - (C - 1) / 2.0
    centred_y = (column_index % C).astype(float_type) - (C - 1) / 2.0
    block_power_real, block_power_imaginary = complex_powers(centred_x[:, None, None] + offset_x, centred_y[None, :, None] + offset_y, ORDER)

    def block_sum(values):
        summed = jnp.sum((strength[..., None] * values).reshape(N_SLAB, C, N_LEAF, C, P_SIZE, ORDER), axis=(1, 3, 4))
        return summed.reshape(N_SLAB * N_LEAF, ORDER)

    block_real = block_sum(block_power_real)
    block_imaginary = block_sum(block_power_imaginary)

    mask_float = near_mask.astype(float_type)
    padded = jnp.pad(particles, ((0, 0), (2, 2), (2, 2), (0, 0)))
    sum_real = jnp.zeros((GX, GY, P_SIZE), float_type)
    sum_imaginary = jnp.zeros((GX, GY, P_SIZE), float_type)
    for number, (step_x, step_y) in enumerate(inner_steps + cycle_steps):
        source = padded[:, 2 + step_x:2 + step_x + GX, 2 + step_y:2 + step_y + GY, :]
        if number < 9:
            circulation = source[2]
        else:
            circulation = source[2] * mask_float[number - 9][..., None]
        near_real, near_imaginary = lax.map(partial(pair_row, step_x, step_y), (offset_x, offset_y, source[0], source[1], circulation))
        sum_real = sum_real + near_real
        sum_imaginary = sum_imaginary + near_imaginary

    margin = 2 * C - 1
    padded_real = jnp.pad(leaf_real, ((margin, margin), (margin, margin), (0, 0)))
    padded_imaginary = jnp.pad(leaf_imaginary, ((margin, margin), (margin, margin), (0, 0)))
    local_real = jnp.zeros((GX, GY, ORDER), float_type)
    local_imaginary = jnp.zeros((GX, GY, ORDER), float_type)
    for number, (step_x, step_y) in enumerate(cycle_steps):
        source_real = padded_real[margin + step_x:margin + step_x + GX, margin + step_y:margin + step_y + GY, :]
        source_imaginary = padded_imaginary[margin + step_x:margin + step_x + GX, margin + step_y:margin + step_y + GY, :]
        matrix_real, matrix_imaginary = translation(jnp.asarray(float(step_x), float_type), jnp.asarray(float(step_y), float_type))
        part_real, part_imaginary = apply_translation(matrix_real, matrix_imaginary, source_real, source_imaginary)
        weight = (1.0 - mask_float[number])[..., None]
        local_real = local_real + weight * part_real
        local_imaginary = local_imaginary + weight * part_imaginary

    far_table = np.array([(a, b) for a in range(-margin, margin + 1) for b in range(-margin, margin + 1) if max(abs(a), abs(b)) >= 3], dtype=np.int32)

    def far_step(totals, offset):
        source_real = lax.dynamic_slice(padded_real, (margin + offset[0], margin + offset[1], jnp.int32(0)), (GX, GY, ORDER))
        source_imaginary = lax.dynamic_slice(padded_imaginary, (margin + offset[0], margin + offset[1], jnp.int32(0)), (GX, GY, ORDER))
        near_rows = jnp.abs((row_index + offset[0]) // C - row_block) <= 1
        near_columns = jnp.abs((column_index + offset[1]) // C - column_block) <= 1
        adjacent = (near_rows[:, None] & near_columns[None, :]).astype(float_type)[..., None]
        matrix_real, matrix_imaginary = translation(offset[0].astype(float_type), offset[1].astype(float_type))
        part_real, part_imaginary = apply_translation(matrix_real, matrix_imaginary, source_real, source_imaginary)
        return (totals[0] + adjacent * part_real, totals[1] + adjacent * part_imaginary), None

    (local_real, local_imaginary), unused = lax.scan(far_step, (local_real, local_imaginary), jnp.asarray(far_table))

    def block_step(totals, pieces):
        index, multipole_real, multipole_imaginary = pieces
        block_x = index // N_LEAF
        block_y = index % N_LEAF
        shift_real = (block_x * C).astype(float_type) + (C - 1) / 2.0 - row_index.astype(float_type)
        shift_imaginary = (block_y * C).astype(float_type) + (C - 1) / 2.0 - column_index.astype(float_type)
        remote = jnp.maximum(jnp.abs(block_x - row_block)[:, None], jnp.abs(block_y - column_block)[None, :]) >= 2
        shift_real = jnp.where(remote, shift_real[:, None], 1.0)
        shift_imaginary = jnp.where(remote, shift_imaginary[None, :], 1.0)
        matrix_real, matrix_imaginary = translation(shift_real, shift_imaginary)
        part_real, part_imaginary = apply_translation(matrix_real, matrix_imaginary, multipole_real, multipole_imaginary)
        weight = remote.astype(float_type)[..., None]
        return (totals[0] + weight * part_real, totals[1] + weight * part_imaginary), None

    (local_real, local_imaginary), unused = lax.scan(block_step, (local_real, local_imaginary), (jnp.arange(N_SLAB * N_LEAF, dtype=jnp.int32), block_real, block_imaginary))

    sum_real = sum_real + jnp.sum(local_real[:, :, None, :] * power_real - local_imaginary[:, :, None, :] * power_imaginary, -1)
    sum_imaginary = sum_imaginary + jnp.sum(local_real[:, :, None, :] * power_imaginary + local_imaginary[:, :, None, :] * power_real, -1)
    return jnp.stack([sum_imaginary, sum_real]) / TWO_PI
```

```python
import functools
import math

import jax
import jax.numpy as jnp
import numpy as np
from jax import lax
from jax.experimental import pallas as pl
from jax.experimental.pallas import tpu as pltpu
from jax.sharding import PartitionSpec as P

ORDER = 10
DELTA_SQUARED = 0.0025
TWO_PI = 2.0 * math.pi
MESH = pl.DeviceIdType.MESH
CYCLE = [(a, b) for a in range(-2, 3) for b in range(-2, 3) if max(abs(a), abs(b)) == 2]
DIRECTIONS = [(a, b) for a in (-1, 0, 1) for b in (-1, 0, 1) if (a, b) != (0, 0)]
WIDTH = 2
FEATURES = 64
CHUNK = 64
MULTI = 24


def span(step, side):
    return {-1: (0, WIDTH), 0: (0, side), 1: (side - WIDTH, WIDTH)}[step]


def landing(step, side):
    return {1: 0, 0: WIDTH, -1: WIDTH + side}[step]


def moment_columns(base_x, base_y, strength, lane):
    power_x, power_y = strength, jnp.zeros_like(strength)
    out = jnp.zeros(lane.shape, jnp.float32)
    for k in range(ORDER):
        if k:
            power_x, power_y = (
                power_x * base_x - power_y * base_y,
                power_x * base_y + power_y * base_x,
            )
        out = jnp.where(lane == k, jnp.sum(power_x, axis=1, keepdims=True), out)
        if k:
            out = jnp.where(lane == ORDER + k, jnp.sum(power_y, axis=1, keepdims=True), out)
    return out


def exchange_kernel(slabs, leaves, side, *refs):
    part_ref, win_ref, own_ref, near_ref, block_ref = refs[:5]
    sends, recvs = refs[5:13], refs[13:21]
    multi_ref, row_ref = refs[21:23]
    halo_send, halo_recv, multi_send, multi_recv, row_send, row_recv = refs[23:]
    count = slabs * leaves
    window = side + 2 * WIDTH
    slab, leaf = lax.axis_index("slab"), lax.axis_index("leaf")
    me = slab * leaves + leaf

    def place(number):
        return (number // leaves, lax.rem(number, leaves))

    barrier = pltpu.get_barrier_semaphore()

    @pl.loop(1, count)
    def _(o):
        pl.semaphore_signal(
            barrier, inc=1, device_id=place(lax.rem(me + o, count)), device_id_type=MESH
        )

    for c in range(3):
        for i in range(side):
            own_ref[c, i * side : (i + 1) * side, :] = part_ref[c, i]
    win_ref[...] = jnp.zeros_like(win_ref)
    for c in range(3):
        for i in range(side):
            at = (i + WIDTH) * window + WIDTH
            win_ref[c, at : at + side, :] = part_ref[c, i]
    for k, (a, b) in enumerate(DIRECTIONS):
        (i0, ni), (j0, nj) = span(a, side), span(b, side)
        for c in range(3):
            for r in range(ni):
                sends[k][c, r * nj : (r + 1) * nj, :] = part_ref[c, i0 + r, j0 : j0 + nj, :]

    def exists(a, b):
        s, l = slab + a, leaf + b
        return (s >= 0) & (s < slabs) & (l >= 0) & (l < leaves)

    def halo_copy(k):
        a, b = DIRECTIONS[k]
        return pltpu.make_async_remote_copy(
            src_ref=sends[k], dst_ref=recvs[k],
            send_sem=halo_send.at[k], recv_sem=halo_recv.at[k],
            device_id=(slab + a, leaf + b), device_id_type=MESH,
        )

    def multi_copy(k):
        a, b = DIRECTIONS[k]
        return pltpu.make_async_remote_copy(
            src_ref=multi_ref, dst_ref=near_ref.at[(1 - a) * 3 + (1 - b)],
            send_sem=multi_send.at[k], recv_sem=multi_recv.at[k],
            device_id=(slab + a, leaf + b), device_id_type=MESH,
        )

    def row_copy(o):
        return pltpu.make_async_remote_copy(
            src_ref=row_ref, dst_ref=block_ref.at[me],
            send_sem=row_send.at[o], recv_sem=row_recv.at[o],
            device_id=place(lax.rem(me + o, count)), device_id_type=MESH,
        )

    pl.semaphore_wait(barrier, count - 1)
    for k, (a, b) in enumerate(DIRECTIONS):
        @pl.when(exists(a, b))
        def _(k=k):
            halo_copy(k).start()

    own_x, own_y, strength = own_ref[0], own_ref[1], own_ref[2]
    lane = lax.broadcasted_iota(jnp.int32, (side * side, 128), 1)
    number = lax.broadcasted_iota(jnp.int32, own_x.shape, 0)
    centred_x = (number // side).astype(jnp.float32) - (side - 1) / 2.0
    centred_y = (number % side).astype(jnp.float32) - (side - 1) / 2.0
    block = moment_columns(own_x + centred_x, own_y + centred_y, strength, lane)
    row_ref[...] = jnp.sum(block, axis=0, keepdims=True)
    block_ref[me] = row_ref[...]

    @pl.loop(1, count)
    def _(o):
        row_copy(o).start()

    columns = moment_columns(own_x, own_y, strength, lane)
    square = jnp.concatenate(
        [columns, jnp.zeros((128 - side * side, 128), jnp.float32)], axis=0
    )
    multi_ref[...] = square.T[:MULTI]
    near_ref[4] = multi_ref[...]
    for k, (a, b) in enumerate(DIRECTIONS):
        @pl.when(exists(a, b))
        def _(k=k):
            multi_copy(k).start()

        @pl.when(jnp.logical_not(exists(-a, -b)))
        def _(a=a, b=b):
            near_ref[(1 - a) * 3 + (1 - b)] = jnp.zeros((MULTI, 128), jnp.float32)

    for k, (a, b) in enumerate(DIRECTIONS):
        @pl.when(exists(-a, -b))
        def _(k=k, a=a, b=b):
            halo_copy(k).wait_recv()
            (i0, ni), (j0, nj) = span(a, side), span(b, side)
            for c in range(3):
                for r in range(ni):
                    at = (landing(a, side) + r) * window + landing(b, side)
                    win_ref[c, at : at + nj, :] = recvs[k][c, r * nj : (r + 1) * nj, :]
            multi_copy(k).wait_recv()

        @pl.when(exists(a, b))
        def _(k=k):
            halo_copy(k).wait_send()
            multi_copy(k).wait_send()

    @pl.loop(1, count)
    def _(o):
        row_copy(o).wait_recv()
        row_copy(o).wait_send()


def rounded(values):
    return values.astype(jnp.bfloat16).astype(jnp.float32)


def pieces(value, extra):
    coarse = jnp.floor(value * 32.0 + 0.5) * (1.0 / 32.0)
    rest = value - coarse
    rest_1 = rounded(rest)
    rest_2 = rounded(rest - rest_1)
    rest = rest_1 + rest_2
    square = coarse * coarse
    square_1 = rounded(square)
    square_2 = square - square_1
    cross = 2.0 * coarse * rest + (rest * rest + extra)
    cross_1 = rounded(cross)
    cross_2 = rounded(cross - cross_1)
    cross_3 = cross - cross_1 - cross_2
    return dict(
        one=jnp.ones_like(value), h=coarse, l1=rest_1, l2=rest_2, s1=square_1, s2=square_2,
        c1=cross_1, c2=cross_2, c3=cross_3,
    )


STEP_HIGH = [("h", -2.0, "one", 1), ("one", 2.0, "h", 1), ("one", 1.0, "one", 2)]
STEP_LOW = [
    ("l1", -2.0, "one", 1), ("l2", -2.0, "one", 1), ("one", 2.0, "l1", 1), ("one", 2.0, "l2", 1),
]
PLAIN_HIGH = [
    ("s1", 1.0, "one", 0), ("s2", 1.0, "one", 0), ("one", 1.0, "s1", 0), ("one", 1.0, "s2", 0),
    ("h", -2.0, "h", 0),
]
PLAIN_LOW = [
    ("c1", 1.0, "one", 0), ("c2", 1.0, "one", 0), ("c3", 1.0, "one", 0),
    ("one", 1.0, "c1", 0), ("one", 1.0, "c2", 0), ("one", 1.0, "c3", 0),
    ("h", -2.0, "l1", 0), ("h", -2.0, "l2", 0), ("l1", -2.0, "h", 0), ("l2", -2.0, "h", 0),
    ("l1", -2.0, "l1", 0), ("l1", -2.0, "l2", 0), ("l2", -2.0, "l1", 0),
]


def both(rows):
    return [(axis, row) for axis in (0, 1) for row in rows]


HIGH = both(STEP_HIGH) + both(PLAIN_HIGH)
ROWS = HIGH + both(STEP_LOW) + both(PLAIN_LOW)


def step_scales():
    table = np.ones((25, 16, 128), np.float32)
    for number in range(25):
        step = (number // 5 - 2, number % 5 - 2)
        for at, first in ((0, 0), (8, 16)):
            for r in range(8):
                axis, (_, _, _, power) = ROWS[first + r]
                table[number, at + r] = float(step[axis]) ** power
    return table


def field_kernel(
    slabs, leaves, side, mask_ref, win_ref, own_ref, near_ref, block_ref, columns_ref, scale_ref,
    out_ref, source_ref, target_ref, left_ref, right_ref, gain_ref, acc_ref, sum_ref,
):
    count = slabs * leaves
    window = side + 2 * WIDTH
    own = side * side
    particles = own_ref.shape[2]
    halves = particles // 128
    all_leaves = window * window

    def fill(ref, get, leaf_count, side_of):
        for g in range(leaf_count // 8):
            for half in range(halves):
                lanes = slice(half * 128, (half + 1) * 128)
                extra = DELTA_SQUARED / 2.0 if side_of == 0 else 0.0
                parts = [pieces(get(c, g, lanes), extra) for c in range(2)]
                for r in range(FEATURES):
                    if r < len(ROWS):
                        axis, (target, factor, source, _) = ROWS[r]
                        if side_of == 0:
                            value = parts[axis][target] * factor
                        else:
                            value = parts[axis][source]
                    else:
                        value = jnp.zeros((8, 128), jnp.float32)
                    ref[half, r * leaf_count + g * 8 : r * leaf_count + g * 8 + 8, :] = value

    fill(target_ref, lambda c, g, lanes: own_ref[c, g * 8 : g * 8 + 8, lanes], own, 0)
    fill(source_ref, lambda c, g, lanes: win_ref[c, g * 8 : g * 8 + 8, lanes], all_leaves, 1)

    @pl.loop(0, own)
    def _(t):
        ti, tj = t // side, lax.rem(t, side)
        for half in range(halves):
            rows = target_ref[half, pl.ds(t, FEATURES, stride=own), :]
            left_ref[half * 128 : (half + 1) * 128, :] = rows.T.astype(jnp.bfloat16)
        for number in range(25):
            dx, dy = number // 5 - 2, number % 5 - 2
            leaf = (ti + (dx + 2)) * window + tj + (dy + 2)
            for half in range(halves):
                lanes = slice(half * 128, (half + 1) * 128)
                base = source_ref[half, pl.ds(leaf, FEATURES, stride=all_leaves), :]
                scale = scale_ref[number]
                base = jnp.concatenate(
                    [base[:8] * scale[:8], base[8:16], base[16:24] * scale[8:], base[24:]], axis=0
                )
                right_ref[number, :, lanes] = base.astype(jnp.bfloat16)
            strength = win_ref[2, pl.ds(leaf, 1), :]
            if max(abs(dx), abs(dy)) == 2:
                strength = strength * mask_ref[CYCLE.index((dx, dy)), ti, tj].astype(jnp.float32)
            gain_ref[number, 0:1, :] = strength
            gain_ref[number, 1:2, :] = strength * (win_ref[0, pl.ds(leaf, 1), :] + float(dx))
            gain_ref[number, 2:3, :] = strength * (win_ref[1, pl.ds(leaf, 1), :] + float(dy))

        @pl.loop(0, particles // CHUNK)
        def _(chunk):
            at = pl.multiple_of(chunk * CHUNK, CHUNK)
            left = left_ref[pl.ds(at, CHUNK), :]
            totals = [jnp.zeros((CHUNK, 128), jnp.float32) for _ in range(3)]
            for number in range(25):
                distance = jnp.dot(
                    left, right_ref[number], preferred_element_type=jnp.float32
                )
                inverse = pl.reciprocal(distance, approx=True)
                for half in range(halves):
                    lanes = slice(half * 128, (half + 1) * 128)
                    part = inverse[:, lanes]
                    for q in range(3):
                        totals[q] = totals[q] + part * gain_ref[number, q : q + 1, lanes]
            for q in range(3):
                acc_ref[q, pl.ds(at, CHUNK), :] = totals[q]

        for q in range(3):
            sum_ref[q, pl.ds(t, 1), :] = jnp.concatenate(
                [
                    jnp.sum(acc_ref[q, half * 128 : (half + 1) * 128, :].T, axis=0, keepdims=True)
                    for half in range(halves)
                ],
                axis=1,
            )

    slab, leaf = lax.axis_index("slab"), lax.axis_index("leaf")
    in_window = 9 * own
    rows = block_ref[:, 0, :]
    block_lanes = -(-count // 128) * 128
    if block_lanes > count:
        rows = jnp.concatenate(
            [rows, jnp.zeros((block_lanes - count, 128), jnp.float32)], axis=0
        )
    blocks = jnp.concatenate(
        [rows[k * 128 : (k + 1) * 128].T[:MULTI] for k in range(block_lanes // 128)], axis=1
    )
    near_lane = lax.broadcasted_iota(jnp.int32, (MULTI, 128), 1)
    groups = -(-in_window // 128)
    parts = [jnp.zeros((MULTI, 128), jnp.float32) for _ in range(groups)]
    for d in range(9):
        piece = jnp.where(near_lane < own, near_ref[d], 0.0)
        at = d * own
        shift = at % 128
        if shift:
            piece = pltpu.roll(piece, shift, 1)
        parts[at // 128] = parts[at // 128] + piece
    used = in_window % 128
    if used and used + count <= 128:
        first_block = in_window
        parts[-1] = parts[-1] + pltpu.roll(blocks[:, :128], used, 1)
    else:
        first_block = groups * 128
        parts.append(blocks)
    moments = jnp.concatenate(parts, axis=1)
    total_lanes = moments.shape[1]

    lane = lax.broadcasted_iota(jnp.int32, (own, total_lanes), 1)
    row = lax.broadcasted_iota(jnp.int32, (own, total_lanes), 0)
    ti, tj = row // side, row % side
    device = lane // own
    inside = lane % own
    dx = (device // 3 - 1) * side + inside // side - ti
    dy = (device % 3 - 1) * side + inside % side - tj
    reach = jnp.maximum(jnp.abs(dx), jnp.abs(dy))
    weight = jnp.zeros((own, total_lanes), jnp.float32)
    for o, (a, b) in enumerate(CYCLE):
        weight = jnp.where((dx == a) & (dy == b), 1.0 - columns_ref[:, o : o + 1], weight)
    weight = jnp.where(reach >= 3, 1.0, weight)
    weight = jnp.where(lane < in_window, weight, 0.0)
    number = lane - first_block
    block_x, block_y = number // leaves, number % leaves
    remote = (number >= 0) & (number < count) & (
        jnp.maximum(jnp.abs(block_x - slab), jnp.abs(block_y - leaf)) >= 2
    )
    middle = (side - 1) / 2.0
    far_x = ((block_x - slab) * side - ti).astype(jnp.float32) + middle
    far_y = ((block_y - leaf) * side - tj).astype(jnp.float32) + middle
    weight = jnp.where(remote, 1.0, weight)
    shift_x = jnp.where(remote, far_x, dx.astype(jnp.float32))
    shift_y = jnp.where(remote, far_y, dy.astype(jnp.float32))
    shift_x = jnp.where(weight == 0.0, 1.0, shift_x)
    shift_y = jnp.where(weight == 0.0, 0.0, shift_y)
    denominator = shift_x * shift_x + shift_y * shift_y
    base_x, base_y = shift_x / denominator, -shift_y / denominator
    power_x, power_y = [weight * base_x], [weight * base_y]
    for n in range(1, 2 * ORDER - 1):
        last_x, last_y = power_x[-1] * float(n), power_y[-1] * float(n)
        power_x.append(last_x * base_x - last_y * base_y)
        power_y.append(last_x * base_y + last_y * base_x)
    local_x, local_y = [], []
    moment_x = [
        moments[k : k + 1] * ((-1.0) ** (k + 1) / math.factorial(k)) for k in range(ORDER)
    ]
    moment_y = [
        moments[ORDER + k : ORDER + k + 1] * ((-1.0) ** (k + 1) / math.factorial(k))
        for k in range(ORDER)
    ]
    for m in range(ORDER):
        sum_x = jnp.zeros((own, total_lanes), jnp.float32)
        sum_y = jnp.zeros((own, total_lanes), jnp.float32)
        for k in range(ORDER):
            px, py = power_x[m + k], power_y[m + k]
            sum_x = sum_x + (moment_x[k] * px - moment_y[k] * py)
            sum_y = sum_y + (moment_x[k] * py + moment_y[k] * px)
        scale = 1.0 / math.factorial(m)
        local_x.append(jnp.sum(sum_x, axis=1, keepdims=True) * scale)
        local_y.append(jnp.sum(sum_y, axis=1, keepdims=True) * scale)

    own_x, own_y = own_ref[0], own_ref[1]
    field_x = jnp.broadcast_to(local_x[-1], own_x.shape)
    field_y = jnp.broadcast_to(local_y[-1], own_x.shape)
    for m in range(ORDER - 2, -1, -1):
        field_x, field_y = (
            field_x * own_x - field_y * own_y + local_x[m],
            field_x * own_y + field_y * own_x + local_y[m],
        )
    first = (sum_ref[2] - own_y * sum_ref[0] + field_y) * (1.0 / TWO_PI)
    second = (own_x * sum_ref[0] - sum_ref[1] + field_x) * (1.0 / TWO_PI)
    for i in range(side):
        out_ref[0, i] = first[i * side : (i + 1) * side]
        out_ref[1, i] = second[i * side : (i + 1) * side]


def body(particles, near_mask, *, slabs, leaves):
    side, count = particles.shape[1], particles.shape[3]
    own = side * side
    window = side + 2 * WIDTH
    devices = slabs * leaves
    f32 = jnp.float32
    vmem = pl.BlockSpec(memory_space=pltpu.VMEM)
    smem = pl.BlockSpec(memory_space=pltpu.SMEM)
    strips = [
        pltpu.VMEM((3, span(a, side)[1] * span(b, side)[1], count), f32) for a, b in DIRECTIONS
    ]
    win, own_part, near, blocks = pl.pallas_call(
        functools.partial(exchange_kernel, slabs, leaves, side),
        out_shape=(
            jax.ShapeDtypeStruct((3, window * window, count), f32),
            jax.ShapeDtypeStruct((3, own, count), f32),
            jax.ShapeDtypeStruct((9, MULTI, 128), f32),
            jax.ShapeDtypeStruct((devices, 1, 128), f32),
        ),
        in_specs=[vmem],
        out_specs=(vmem, vmem, vmem, vmem),
        scratch_shapes=strips + strips + [
            pltpu.VMEM((MULTI, 128), f32),
            pltpu.VMEM((1, 128), f32),
            pltpu.SemaphoreType.DMA((8,)), pltpu.SemaphoreType.DMA((8,)),
            pltpu.SemaphoreType.DMA((8,)), pltpu.SemaphoreType.DMA((8,)),
            pltpu.SemaphoreType.DMA((devices,)), pltpu.SemaphoreType.DMA((devices,)),
        ],
        compiler_params=pltpu.CompilerParams(collective_id=0, has_side_effects=True),
        name="exchange",
    )(particles)
    columns = near_mask.reshape(len(CYCLE), own).T.astype(f32)
    bf16 = jnp.bfloat16
    return pl.pallas_call(
        functools.partial(field_kernel, slabs, leaves, side),
        out_shape=jax.ShapeDtypeStruct((2, side, side, count), f32),
        in_specs=[smem] + [vmem] * 6,
        out_specs=vmem,
        scratch_shapes=[
            pltpu.VMEM((count // 128, FEATURES * window * window, 128), f32),
            pltpu.VMEM((count // 128, FEATURES * own, 128), f32),
            pltpu.VMEM((count, FEATURES), bf16),
            pltpu.VMEM((25, FEATURES, count), bf16),
            pltpu.VMEM((25, 8, count), f32),
            pltpu.VMEM((3, count, 128), f32),
            pltpu.VMEM((3, own, count), f32),
        ],
        compiler_params=pltpu.CompilerParams(vmem_limit_bytes=48 * 1024 * 1024),
        name="field",
    )(near_mask, win, own_part, near, blocks, columns, jnp.asarray(step_scales()))


def solution(mesh):
    return jax.shard_map(
        functools.partial(body, slabs=mesh.shape["slab"], leaves=mesh.shape["leaf"]),
        mesh=mesh,
        in_specs=(P(None, "slab", "leaf", None), P(None, "slab", "leaf")),
        out_specs=P(None, "slab", "leaf", None),
        check_vma=False,
    )
```

```python
import functools
import math

import jax
import jax.numpy as jnp
import numpy as np
from jax import lax
from jax.experimental import pallas as pl
from jax.experimental.pallas import tpu as pltpu
from jax.sharding import PartitionSpec as P

ORDER = 10
DELTA_SQUARED = 0.0025
TWO_PI = 2.0 * math.pi
MESH = pl.DeviceIdType.MESH
CYCLE = [(a, b) for a in range(-2, 3) for b in range(-2, 3) if max(abs(a), abs(b)) == 2]
DIRECTIONS = [(a, b) for a in (-1, 0, 1) for b in (-1, 0, 1) if (a, b) != (0, 0)]
WIDTH = 2
FEATURES = 48
CHUNK = 64
MULTI = 24


def span(step, side):
    return {-1: (0, WIDTH), 0: (0, side), 1: (side - WIDTH, WIDTH)}[step]


def landing(step, side):
    return {1: 0, 0: WIDTH, -1: WIDTH + side}[step]


def moment_columns(base_x, base_y, strength, lane):
    power_x, power_y = strength, jnp.zeros_like(strength)
    out = jnp.zeros(lane.shape, jnp.float32)
    for k in range(ORDER):
        if k:
            power_x, power_y = (
                power_x * base_x - power_y * base_y,
                power_x * base_y + power_y * base_x,
            )
        out = jnp.where(lane == k, jnp.sum(power_x, axis=1, keepdims=True), out)
        if k:
            out = jnp.where(lane == ORDER + k, jnp.sum(power_y, axis=1, keepdims=True), out)
    return out


def exchange_kernel(slabs, leaves, side, *refs):
    part_ref, win_ref, own_ref, near_ref, block_ref = refs[:5]
    sends, recvs = refs[5:13], refs[13:21]
    multi_ref, row_ref = refs[21:23]
    halo_send, halo_recv, multi_send, multi_recv, row_send, row_recv = refs[23:]
    count = slabs * leaves
    window = side + 2 * WIDTH
    slab, leaf = lax.axis_index("slab"), lax.axis_index("leaf")
    me = slab * leaves + leaf

    def place(number):
        return (number // leaves, lax.rem(number, leaves))

    barrier = pltpu.get_barrier_semaphore()

    @pl.loop(1, count)
    def _(o):
        pl.semaphore_signal(
            barrier, inc=1, device_id=place(lax.rem(me + o, count)), device_id_type=MESH
        )

    for c in range(3):
        for i in range(side):
            own_ref[c, i * side : (i + 1) * side, :] = part_ref[c, i]
    win_ref[...] = jnp.zeros_like(win_ref)
    for c in range(3):
        for i in range(side):
            at = (i + WIDTH) * window + WIDTH
            win_ref[c, at : at + side, :] = part_ref[c, i]
    for k, (a, b) in enumerate(DIRECTIONS):
        (i0, ni), (j0, nj) = span(a, side), span(b, side)
        for c in range(3):
            for r in range(ni):
                sends[k][c, r * nj : (r + 1) * nj, :] = part_ref[c, i0 + r, j0 : j0 + nj, :]

    def exists(a, b):
        s, l = slab + a, leaf + b
        return (s >= 0) & (s < slabs) & (l >= 0) & (l < leaves)

    def halo_copy(k):
        a, b = DIRECTIONS[k]
        return pltpu.make_async_remote_copy(
            src_ref=sends[k], dst_ref=recvs[k],
            send_sem=halo_send.at[k], recv_sem=halo_recv.at[k],
            device_id=(slab + a, leaf + b), device_id_type=MESH,
        )

    def multi_copy(k):
        a, b = DIRECTIONS[k]
        return pltpu.make_async_remote_copy(
            src_ref=multi_ref, dst_ref=near_ref.at[(1 - a) * 3 + (1 - b)],
            send_sem=multi_send.at[k], recv_sem=multi_recv.at[k],
            device_id=(slab + a, leaf + b), device_id_type=MESH,
        )

    def row_copy(o):
        return pltpu.make_async_remote_copy(
            src_ref=row_ref, dst_ref=block_ref.at[me],
            send_sem=row_send.at[o], recv_sem=row_recv.at[o],
            device_id=place(lax.rem(me + o, count)), device_id_type=MESH,
        )

    pl.semaphore_wait(barrier, count - 1)
    for k, (a, b) in enumerate(DIRECTIONS):
        @pl.when(exists(a, b))
        def _(k=k):
            halo_copy(k).start()

    own_x, own_y, strength = own_ref[0], own_ref[1], own_ref[2]
    lane = lax.broadcasted_iota(jnp.int32, (side * side, 128), 1)
    number = lax.broadcasted_iota(jnp.int32, own_x.shape, 0)
    centred_x = (number // side).astype(jnp.float32) - (side - 1) / 2.0
    centred_y = (number % side).astype(jnp.float32) - (side - 1) / 2.0
    block = moment_columns(own_x + centred_x, own_y + centred_y, strength, lane)
    row_ref[...] = jnp.sum(block, axis=0, keepdims=True)
    block_ref[me] = row_ref[...]

    @pl.loop(1, count)
    def _(o):
        row_copy(o).start()

    columns = moment_columns(own_x, own_y, strength, lane)
    square = jnp.concatenate(
        [columns, jnp.zeros((128 - side * side, 128), jnp.float32)], axis=0
    )
    multi_ref[...] = square.T[:MULTI]
    near_ref[4] = multi_ref[...]
    for k, (a, b) in enumerate(DIRECTIONS):
        @pl.when(exists(a, b))
        def _(k=k):
            multi_copy(k).start()

        @pl.when(jnp.logical_not(exists(-a, -b)))
        def _(a=a, b=b):
            near_ref[(1 - a) * 3 + (1 - b)] = jnp.zeros((MULTI, 128), jnp.float32)

    for k, (a, b) in enumerate(DIRECTIONS):
        @pl.when(exists(-a, -b))
        def _(k=k, a=a, b=b):
            halo_copy(k).wait_recv()
            (i0, ni), (j0, nj) = span(a, side), span(b, side)
            for c in range(3):
                for r in range(ni):
                    at = (landing(a, side) + r) * window + landing(b, side)
                    win_ref[c, at : at + nj, :] = recvs[k][c, r * nj : (r + 1) * nj, :]
            multi_copy(k).wait_recv()

        @pl.when(exists(a, b))
        def _(k=k):
            halo_copy(k).wait_send()
            multi_copy(k).wait_send()

    @pl.loop(1, count)
    def _(o):
        row_copy(o).wait_recv()
        row_copy(o).wait_send()


def rounded(values):
    return values.astype(jnp.bfloat16).astype(jnp.float32)


def pieces(value, place, extra):
    coarse = jnp.floor(value * 32.0 + 0.5) * (1.0 / 32.0)
    rest = value - coarse
    rest_1 = rounded(rest)
    rest_2 = rounded(rest - rest_1)
    rest = rest_1 + rest_2
    coarse = coarse + place
    square = coarse * coarse
    square_1 = rounded(square)
    square_2 = square - square_1
    cross = 2.0 * coarse * rest + (rest * rest + extra)
    cross_1 = rounded(cross)
    cross_2 = rounded(cross - cross_1)
    cross_3 = cross - cross_1 - cross_2
    return dict(
        one=jnp.ones_like(value), h=coarse, l1=rest_1, l2=rest_2, s1=square_1, s2=square_2,
        c1=cross_1, c2=cross_2, c3=cross_3,
    )


HIGH = [
    ("s1", 1.0, "one"), ("s2", 1.0, "one"), ("one", 1.0, "s1"), ("one", 1.0, "s2"),
    ("h", -2.0, "h"),
]
LOW = [
    ("c1", 1.0, "one"), ("c2", 1.0, "one"), ("c3", 1.0, "one"),
    ("one", 1.0, "c1"), ("one", 1.0, "c2"), ("one", 1.0, "c3"),
    ("h", -2.0, "l1"), ("h", -2.0, "l2"), ("l1", -2.0, "h"), ("l2", -2.0, "h"),
    ("l1", -2.0, "l1"), ("l1", -2.0, "l2"), ("l2", -2.0, "l1"),
]
ROWS = [(axis, row) for rows in (HIGH, LOW) for axis in (0, 1) for row in rows]


def field_kernel(
    slabs, leaves, side, mask_ref, win_ref, own_ref, near_ref, block_ref, columns_ref,
    out_ref, source_ref, target_ref, left_ref, right_ref, gain_ref, acc_ref, sum_ref,
):
    count = slabs * leaves
    window = side + 2 * WIDTH
    own = side * side
    particles = own_ref.shape[2]
    halves = particles // 128
    all_leaves = window * window

    def fill(ref, get, width, is_target):
        leaf_count = width * width
        stride = leaf_count + 8
        index = lax.broadcasted_iota(jnp.int32, (8, 128), 0)
        low = 0 if is_target else WIDTH
        for g in range(leaf_count // 8):
            place_x = ((index + g * 8) // width - low).astype(jnp.float32) - (side - 1) / 2.0
            place_y = ((index + g * 8) % width - low).astype(jnp.float32) - (side - 1) / 2.0
            for half in range(halves):
                lanes = slice(half * 128, (half + 1) * 128)
                extra = DELTA_SQUARED / 2.0 if is_target else 0.0
                parts = [
                    pieces(get(c, g, lanes), place, extra)
                    for c, place in ((0, place_x), (1, place_y))
                ]
                for r in range(FEATURES):
                    if r < len(ROWS):
                        axis, (target, factor, source) = ROWS[r]
                        value = parts[axis][target] * factor if is_target else parts[axis][source]
                    else:
                        value = jnp.zeros((8, 128), jnp.float32)
                    ref[half, r * stride + g * 8 : r * stride + g * 8 + 8, :] = value

    fill(target_ref, lambda c, g, lanes: own_ref[c, g * 8 : g * 8 + 8, lanes], side, True)
    fill(source_ref, lambda c, g, lanes: win_ref[c, g * 8 : g * 8 + 8, lanes], window, False)

    @pl.loop(0, all_leaves)
    def _(leaf):
        for half in range(halves):
            lanes = slice(half * 128, (half + 1) * 128)
            rows = source_ref[half, pl.ds(leaf, FEATURES, stride=all_leaves + 8), :]
            right_ref[leaf, :, lanes] = rows.astype(jnp.bfloat16)

    @pl.loop(0, own)
    def _(t):
        ti, tj = t // side, lax.rem(t, side)
        for half in range(halves):
            rows = target_ref[half, pl.ds(t, FEATURES, stride=own + 8), :]
            left_ref[half * 128 : (half + 1) * 128, :] = rows.T.astype(jnp.bfloat16)
        for number in range(25):
            dx, dy = number // 5 - 2, number % 5 - 2
            leaf = (ti + (dx + 2)) * window + tj + (dy + 2)
            strength = win_ref[2, pl.ds(leaf, 1), :]
            if max(abs(dx), abs(dy)) == 2:
                strength = strength * mask_ref[CYCLE.index((dx, dy)), ti, tj].astype(jnp.float32)
            gain_ref[number, 0:1, :] = strength
            gain_ref[number, 1:2, :] = strength * (win_ref[0, pl.ds(leaf, 1), :] + float(dx))
            gain_ref[number, 2:3, :] = strength * (win_ref[1, pl.ds(leaf, 1), :] + float(dy))

        @pl.loop(0, particles // CHUNK)
        def _(chunk):
            at = pl.multiple_of(chunk * CHUNK, CHUNK)
            left = left_ref[pl.ds(at, CHUNK), :]
            totals = [jnp.zeros((CHUNK, 128), jnp.float32) for _ in range(3)]
            for number in range(25):
                leaf = (ti + number // 5) * window + tj + number % 5
                distance = jnp.dot(left, right_ref[leaf], preferred_element_type=jnp.float32)
                inverse = pl.reciprocal(distance, approx=True)
                for half in range(halves):
                    lanes = slice(half * 128, (half + 1) * 128)
                    part = inverse[:, lanes]
                    for q in range(3):
                        totals[q] = totals[q] + part * gain_ref[number, q : q + 1, lanes]
            for q in range(3):
                acc_ref[q, pl.ds(at, CHUNK), :] = totals[q]

        for q in range(3):
            sum_ref[q, pl.ds(t, 1), :] = jnp.concatenate(
                [
                    jnp.sum(acc_ref[q, half * 128 : (half + 1) * 128, :].T, axis=0, keepdims=True)
                    for half in range(halves)
                ],
                axis=1,
            )

    slab, leaf = lax.axis_index("slab"), lax.axis_index("leaf")
    in_window = 9 * own
    rows = block_ref[:, 0, :]
    block_lanes = -(-count // 128) * 128
    if block_lanes > count:
        rows = jnp.concatenate(
            [rows, jnp.zeros((block_lanes - count, 128), jnp.float32)], axis=0
        )
    blocks = jnp.concatenate(
        [rows[k * 128 : (k + 1) * 128].T[:MULTI] for k in range(block_lanes // 128)], axis=1
    )
    near_lane = lax.broadcasted_iota(jnp.int32, (MULTI, 128), 1)
    groups = -(-in_window // 128)
    parts = [jnp.zeros((MULTI, 128), jnp.float32) for _ in range(groups)]
    for d in range(9):
        piece = jnp.where(near_lane < own, near_ref[d], 0.0)
        at = d * own
        shift = at % 128
        if shift:
            piece = pltpu.roll(piece, shift, 1)
        parts[at // 128] = parts[at // 128] + piece
    used = in_window % 128
    if used and used + count <= 128:
        first_block = in_window
        parts[-1] = parts[-1] + pltpu.roll(blocks[:, :128], used, 1)
    else:
        first_block = groups * 128
        parts.append(blocks)
    moments = jnp.concatenate(parts, axis=1)
    total_lanes = moments.shape[1]

    lane = lax.broadcasted_iota(jnp.int32, (own, total_lanes), 1)
    row = lax.broadcasted_iota(jnp.int32, (own, total_lanes), 0)
    ti, tj = row // side, row % side
    device = lane // own
    inside = lane % own
    dx = (device // 3 - 1) * side + inside // side - ti
    dy = (device % 3 - 1) * side + inside % side - tj
    reach = jnp.maximum(jnp.abs(dx), jnp.abs(dy))
    weight = jnp.zeros((own, total_lanes), jnp.float32)
    for o, (a, b) in enumerate(CYCLE):
        weight = jnp.where((dx == a) & (dy == b), 1.0 - columns_ref[:, o : o + 1], weight)
    weight = jnp.where(reach >= 3, 1.0, weight)
    weight = jnp.where(lane < in_window, weight, 0.0)
    number = lane - first_block
    block_x, block_y = number // leaves, number % leaves
    remote = (number >= 0) & (number < count) & (
        jnp.maximum(jnp.abs(block_x - slab), jnp.abs(block_y - leaf)) >= 2
    )
    middle = (side - 1) / 2.0
    far_x = ((block_x - slab) * side - ti).astype(jnp.float32) + middle
    far_y = ((block_y - leaf) * side - tj).astype(jnp.float32) + middle
    weight = jnp.where(remote, 1.0, weight)
    shift_x = jnp.where(remote, far_x, dx.astype(jnp.float32))
    shift_y = jnp.where(remote, far_y, dy.astype(jnp.float32))
    shift_x = jnp.where(weight == 0.0, 1.0, shift_x)
    shift_y = jnp.where(weight == 0.0, 0.0, shift_y)
    denominator = shift_x * shift_x + shift_y * shift_y
    base_x, base_y = shift_x / denominator, -shift_y / denominator
    power_x, power_y = [weight * base_x], [weight * base_y]
    for n in range(1, 2 * ORDER - 1):
        last_x, last_y = power_x[-1] * float(n), power_y[-1] * float(n)
        power_x.append(last_x * base_x - last_y * base_y)
        power_y.append(last_x * base_y + last_y * base_x)
    local_x, local_y = [], []
    moment_x = [
        moments[k : k + 1] * ((-1.0) ** (k + 1) / math.factorial(k)) for k in range(ORDER)
    ]
    moment_y = [
        moments[ORDER + k : ORDER + k + 1] * ((-1.0) ** (k + 1) / math.factorial(k))
        for k in range(ORDER)
    ]
    for m in range(ORDER):
        sum_x = jnp.zeros((own, total_lanes), jnp.float32)
        sum_y = jnp.zeros((own, total_lanes), jnp.float32)
        for k in range(ORDER):
            px, py = power_x[m + k], power_y[m + k]
            sum_x = sum_x + (moment_x[k] * px - moment_y[k] * py)
            sum_y = sum_y + (moment_x[k] * py + moment_y[k] * px)
        scale = 1.0 / math.factorial(m)
        local_x.append(jnp.sum(sum_x, axis=1, keepdims=True) * scale)
        local_y.append(jnp.sum(sum_y, axis=1, keepdims=True) * scale)

    own_x, own_y = own_ref[0], own_ref[1]
    field_x = jnp.broadcast_to(local_x[-1], own_x.shape)
    field_y = jnp.broadcast_to(local_y[-1], own_x.shape)
    for m in range(ORDER - 2, -1, -1):
        field_x, field_y = (
            field_x * own_x - field_y * own_y + local_x[m],
            field_x * own_y + field_y * own_x + local_y[m],
        )
    first = (sum_ref[2] - own_y * sum_ref[0] + field_y) * (1.0 / TWO_PI)
    second = (own_x * sum_ref[0] - sum_ref[1] + field_x) * (1.0 / TWO_PI)
    for i in range(side):
        out_ref[0, i] = first[i * side : (i + 1) * side]
        out_ref[1, i] = second[i * side : (i + 1) * side]


def body(particles, near_mask, *, slabs, leaves):
    side, count = particles.shape[1], particles.shape[3]
    own = side * side
    window = side + 2 * WIDTH
    devices = slabs * leaves
    f32 = jnp.float32
    vmem = pl.BlockSpec(memory_space=pltpu.VMEM)
    smem = pl.BlockSpec(memory_space=pltpu.SMEM)
    strips = [
        pltpu.VMEM((3, span(a, side)[1] * span(b, side)[1], count), f32) for a, b in DIRECTIONS
    ]
    win, own_part, near, blocks = pl.pallas_call(
        functools.partial(exchange_kernel, slabs, leaves, side),
        out_shape=(
            jax.ShapeDtypeStruct((3, window * window, count), f32),
            jax.ShapeDtypeStruct((3, own, count), f32),
            jax.ShapeDtypeStruct((9, MULTI, 128), f32),
            jax.ShapeDtypeStruct((devices, 1, 128), f32),
        ),
        in_specs=[vmem],
        out_specs=(vmem, vmem, vmem, vmem),
        scratch_shapes=strips + strips + [
            pltpu.VMEM((MULTI, 128), f32),
            pltpu.VMEM((1, 128), f32),
            pltpu.SemaphoreType.DMA((8,)), pltpu.SemaphoreType.DMA((8,)),
            pltpu.SemaphoreType.DMA((8,)), pltpu.SemaphoreType.DMA((8,)),
            pltpu.SemaphoreType.DMA((devices,)), pltpu.SemaphoreType.DMA((devices,)),
        ],
        compiler_params=pltpu.CompilerParams(collective_id=0, has_side_effects=True),
        name="exchange",
    )(particles)
    columns = near_mask.reshape(len(CYCLE), own).T.astype(f32)
    bf16 = jnp.bfloat16
    return pl.pallas_call(
        functools.partial(field_kernel, slabs, leaves, side),
        out_shape=jax.ShapeDtypeStruct((2, side, side, count), f32),
        in_specs=[smem] + [vmem] * 5,
        out_specs=vmem,
        scratch_shapes=[
            pltpu.VMEM((count // 128, FEATURES * (window * window + 8), 128), f32),
            pltpu.VMEM((count // 128, FEATURES * (own + 8), 128), f32),
            pltpu.VMEM((count, FEATURES), bf16),
            pltpu.VMEM((window * window, FEATURES, count), bf16),
            pltpu.VMEM((25, 8, count), f32),
            pltpu.VMEM((3, count, 128), f32),
            pltpu.VMEM((3, own, count), f32),
        ],
        compiler_params=pltpu.CompilerParams(vmem_limit_bytes=48 * 1024 * 1024),
        name="field",
    )(near_mask, win, own_part, near, blocks, columns)


def solution(mesh):
    return jax.shard_map(
        functools.partial(body, slabs=mesh.shape["slab"], leaves=mesh.shape["leaf"]),
        mesh=mesh,
        in_specs=(P(None, "slab", "leaf", None), P(None, "slab", "leaf")),
        out_specs=P(None, "slab", "leaf", None),
        check_vma=False,
    )
```

```python
import functools
import math

import jax
import jax.numpy as jnp
import numpy as np
from jax import lax
from jax.experimental import pallas as pl
from jax.experimental.pallas import tpu as pltpu
from jax.sharding import PartitionSpec as P

ORDER = 10
DELTA_SQUARED = 0.0025
TWO_PI = 2.0 * math.pi
MESH = pl.DeviceIdType.MESH
CYCLE = [(a, b) for a in range(-2, 3) for b in range(-2, 3) if max(abs(a), abs(b)) == 2]
DIRECTIONS = [(a, b) for a in (-1, 0, 1) for b in (-1, 0, 1) if (a, b) != (0, 0)]
WIDTH = 2
FEATURES = 48
CHUNK = 64
MULTI = 24


def span(step, side):
    return {-1: (0, WIDTH), 0: (0, side), 1: (side - WIDTH, WIDTH)}[step]


def landing(step, side):
    return {1: 0, 0: WIDTH, -1: WIDTH + side}[step]


def moment_columns(base_x, base_y, strength, lane):
    power_x, power_y = strength, jnp.zeros_like(strength)
    out = jnp.zeros(lane.shape, jnp.float32)
    for k in range(ORDER):
        if k:
            power_x, power_y = (
                power_x * base_x - power_y * base_y,
                power_x * base_y + power_y * base_x,
            )
        out = jnp.where(lane == k, jnp.sum(power_x, axis=1, keepdims=True), out)
        if k:
            out = jnp.where(lane == ORDER + k, jnp.sum(power_y, axis=1, keepdims=True), out)
    return out


def rounded(values):
    return values.astype(jnp.bfloat16).astype(jnp.float32)


def pieces(value, place, extra):
    coarse = jnp.floor(value * 32.0 + 0.5) * (1.0 / 32.0)
    rest = value - coarse
    rest_1 = rounded(rest)
    rest_2 = rounded(rest - rest_1)
    rest = rest_1 + rest_2
    coarse = coarse + place
    square = coarse * coarse
    square_1 = rounded(square)
    square_2 = square - square_1
    cross = 2.0 * coarse * rest + (rest * rest + extra)
    cross_1 = rounded(cross)
    cross_2 = rounded(cross - cross_1)
    cross_3 = cross - cross_1 - cross_2
    return dict(
        one=jnp.ones_like(value), h=coarse, l1=rest_1, l2=rest_2, s1=square_1, s2=square_2,
        c1=cross_1, c2=cross_2, c3=cross_3,
    )


HIGH = [
    ("s1", 1.0, "one"), ("s2", 1.0, "one"), ("one", 1.0, "s1"), ("one", 1.0, "s2"),
    ("h", -2.0, "h"),
]
LOW = [
    ("c1", 1.0, "one"), ("c2", 1.0, "one"), ("c3", 1.0, "one"),
    ("one", 1.0, "c1"), ("one", 1.0, "c2"), ("one", 1.0, "c3"),
    ("h", -2.0, "l1"), ("h", -2.0, "l2"), ("l1", -2.0, "h"), ("l2", -2.0, "h"),
    ("l1", -2.0, "l1"), ("l1", -2.0, "l2"), ("l2", -2.0, "l1"),
]
ROWS = [(axis, row) for rows in (HIGH, LOW) for axis in (0, 1) for row in rows]


def field_kernel(slabs, leaves, side, mask_ref, part_ref, out_ref, *refs):
    win_ref, own_ref, near_ref, block_ref = refs[:4]
    sends, recvs = refs[4:12], refs[12:20]
    multi_ref, row_ref = refs[20:22]
    halo_send, halo_recv, multi_send, multi_recv, row_send, row_recv = refs[22:28]
    source_ref, target_ref, left_ref, right_ref, gain_ref, acc_ref, sum_ref = refs[28:]
    count = slabs * leaves
    window = side + 2 * WIDTH
    own = side * side
    particles = part_ref.shape[3]
    halves = particles // 128
    all_leaves = window * window
    slab, leaf = lax.axis_index("slab"), lax.axis_index("leaf")
    me = slab * leaves + leaf

    def place(number):
        return (number // leaves, lax.rem(number, leaves))

    barrier = pltpu.get_barrier_semaphore()

    @pl.loop(1, count)
    def _(o):
        pl.semaphore_signal(
            barrier, inc=1, device_id=place(lax.rem(me + o, count)), device_id_type=MESH
        )

    for c in range(3):
        for i in range(side):
            own_ref[c, i * side : (i + 1) * side, :] = part_ref[c, i]
    win_ref[...] = jnp.zeros_like(win_ref)
    for c in range(3):
        for i in range(side):
            at = (i + WIDTH) * window + WIDTH
            win_ref[c, at : at + side, :] = part_ref[c, i]
    for k, (a, b) in enumerate(DIRECTIONS):
        (i0, ni), (j0, nj) = span(a, side), span(b, side)
        for c in range(3):
            for r in range(ni):
                sends[k][c, r * nj : (r + 1) * nj, :] = part_ref[c, i0 + r, j0 : j0 + nj, :]

    def exists(a, b):
        s, l = slab + a, leaf + b
        return (s >= 0) & (s < slabs) & (l >= 0) & (l < leaves)

    def halo_copy(k):
        a, b = DIRECTIONS[k]
        return pltpu.make_async_remote_copy(
            src_ref=sends[k], dst_ref=recvs[k],
            send_sem=halo_send.at[k], recv_sem=halo_recv.at[k],
            device_id=(slab + a, leaf + b), device_id_type=MESH,
        )

    def multi_copy(k):
        a, b = DIRECTIONS[k]
        return pltpu.make_async_remote_copy(
            src_ref=multi_ref, dst_ref=near_ref.at[(1 - a) * 3 + (1 - b)],
            send_sem=multi_send.at[k], recv_sem=multi_recv.at[k],
            device_id=(slab + a, leaf + b), device_id_type=MESH,
        )

    def row_copy(o):
        return pltpu.make_async_remote_copy(
            src_ref=row_ref, dst_ref=block_ref.at[me],
            send_sem=row_send.at[o], recv_sem=row_recv.at[o],
            device_id=place(lax.rem(me + o, count)), device_id_type=MESH,
        )

    pl.semaphore_wait(barrier, count - 1)
    for k, (a, b) in enumerate(DIRECTIONS):
        @pl.when(exists(a, b))
        def _(k=k):
            halo_copy(k).start()

    own_x, own_y, strength = own_ref[0], own_ref[1], own_ref[2]
    lane = lax.broadcasted_iota(jnp.int32, (side * side, 128), 1)
    number = lax.broadcasted_iota(jnp.int32, own_x.shape, 0)
    centred_x = (number // side).astype(jnp.float32) - (side - 1) / 2.0
    centred_y = (number % side).astype(jnp.float32) - (side - 1) / 2.0
    block = moment_columns(own_x + centred_x, own_y + centred_y, strength, lane)
    row_ref[...] = jnp.sum(block, axis=0, keepdims=True)
    block_ref[me] = row_ref[...]

    @pl.loop(1, count)
    def _(o):
        row_copy(o).start()

    columns = moment_columns(own_x, own_y, strength, lane)
    square = jnp.concatenate(
        [columns, jnp.zeros((128 - side * side, 128), jnp.float32)], axis=0
    )
    multi_ref[...] = square.T[:MULTI]
    near_ref[4] = multi_ref[...]
    for k, (a, b) in enumerate(DIRECTIONS):
        @pl.when(exists(a, b))
        def _(k=k):
            multi_copy(k).start()

        @pl.when(jnp.logical_not(exists(-a, -b)))
        def _(a=a, b=b):
            near_ref[(1 - a) * 3 + (1 - b)] = jnp.zeros((MULTI, 128), jnp.float32)

    def fill(ref, get, width, is_target, groups):
        leaf_count = width * width
        stride = leaf_count + 8
        index = lax.broadcasted_iota(jnp.int32, (8, 128), 0)
        low = 0 if is_target else WIDTH
        for g in groups:
            place_x = ((index + g * 8) // width - low).astype(jnp.float32) - (side - 1) / 2.0
            place_y = ((index + g * 8) % width - low).astype(jnp.float32) - (side - 1) / 2.0
            for half in range(halves):
                lanes = slice(half * 128, (half + 1) * 128)
                extra = DELTA_SQUARED / 2.0 if is_target else 0.0
                parts = [
                    pieces(get(c, g, lanes), place, extra)
                    for c, place in ((0, place_x), (1, place_y))
                ]
                for r in range(FEATURES):
                    if r < len(ROWS):
                        axis, (target, factor, source) = ROWS[r]
                        value = parts[axis][target] * factor if is_target else parts[axis][source]
                    else:
                        value = jnp.zeros((8, 128), jnp.float32)
                    ref[half, r * stride + g * 8 : r * stride + g * 8 + 8, :] = value


    def target_leaf(t):
        for half in range(halves):
            rows = target_ref[half, pl.ds(t, FEATURES, stride=own + 8), :]
            left_ref[half * 128 : (half + 1) * 128, :] = rows.T.astype(jnp.bfloat16)

    def source_leaf(number):
        for half in range(halves):
            lanes = slice(half * 128, (half + 1) * 128)
            rows = source_ref[half, pl.ds(number, FEATURES, stride=all_leaves + 8), :]
            right_ref[number, :, lanes] = rows.astype(jnp.bfloat16)

    def pair_sums(t, ti, tj, steps, first):
        target_leaf(t)
        sources = []
        for number, (dx, dy) in enumerate(steps):
            source = (ti + (dx + WIDTH)) * window + tj + (dy + WIDTH)
            sources.append(source)
            strength = win_ref[2, pl.ds(source, 1), :]
            if isinstance(dx, int) and isinstance(dy, int):
                if max(abs(dx), abs(dy)) == 2:
                    o = CYCLE.index((dx, dy))
                    strength = strength * mask_ref[o, ti, tj].astype(jnp.float32)
                shift_x, shift_y = float(dx), float(dy)
            else:
                dx, dy = jnp.int32(dx), jnp.int32(dy)
                o = jnp.where(dx == -2, dy + 2, jnp.where(dx == 2, dy + 13, 7 + 2 * dx))
                o = jnp.where((jnp.abs(dx) < 2) & (dy == 2), o + 1, o)
                o = jnp.maximum(0, jnp.minimum(o, len(CYCLE) - 1))
                outer = jnp.maximum(jnp.abs(dx), jnp.abs(dy)) == 2
                chosen = jnp.where(outer, mask_ref[o, ti, tj], 1)
                strength = strength * chosen.astype(jnp.float32)
                shift_x, shift_y = dx.astype(jnp.float32), dy.astype(jnp.float32)
            gain_ref[number, 0:1, :] = strength
            gain_ref[number, 1:2, :] = strength * (win_ref[0, pl.ds(source, 1), :] + shift_x)
            gain_ref[number, 2:3, :] = strength * (win_ref[1, pl.ds(source, 1), :] + shift_y)

        @pl.loop(0, particles // CHUNK)
        def _(chunk):
            at = pl.multiple_of(chunk * CHUNK, CHUNK)
            left = left_ref[pl.ds(at, CHUNK), :]
            totals = [jnp.zeros((CHUNK, 128), jnp.float32) for _ in range(3)]
            for number, source in enumerate(sources):
                distance = jnp.dot(left, right_ref[source], preferred_element_type=jnp.float32)
                inverse = pl.reciprocal(distance, approx=True)
                for half in range(halves):
                    lanes = slice(half * 128, (half + 1) * 128)
                    part = inverse[:, lanes]
                    for q in range(3):
                        totals[q] = totals[q] + part * gain_ref[number, q : q + 1, lanes]
            for q in range(3):
                acc_ref[q, pl.ds(at, CHUNK), :] = totals[q]

        for q in range(3):
            sums = jnp.concatenate(
                [
                    jnp.sum(acc_ref[q, half * 128 : (half + 1) * 128, :].T, axis=0, keepdims=True)
                    for half in range(halves)
                ],
                axis=1,
            )
            if first:
                sum_ref[q, pl.ds(t, 1), :] = sums
            else:
                sum_ref[q, pl.ds(t, 1), :] = sum_ref[q, pl.ds(t, 1), :] + sums

    def own_rows(c, g, lanes):
        return own_ref[c, g * 8 : g * 8 + 8, lanes]

    def window_rows(c, g, lanes):
        return win_ref[c, g * 8 : g * 8 + 8, lanes]

    fill(target_ref, own_rows, side, True, range(own // 8))
    fill(source_ref, window_rows, window, False, range(WIDTH, WIDTH + side))

    @pl.loop(0, own)
    def _(s):
        source_leaf((s // side + WIDTH) * window + lax.rem(s, side) + WIDTH)

    inner_side = 2 * WIDTH + 2 - side
    inner_low = side - 1 - WIDTH

    @pl.loop(0, inner_side * inner_side)
    def _(n):
        ti, tj = inner_low + n // inner_side, inner_low + lax.rem(n, inner_side)
        steps = [(si - ti, sj - tj) for si in range(side) for sj in range(side)]
        pair_sums(ti * side + tj, ti, tj, steps, True)

    for k, (a, b) in enumerate(DIRECTIONS):
        @pl.when(exists(-a, -b))
        def _(k=k, a=a, b=b):
            halo_copy(k).wait_recv()
            (i0, ni), (j0, nj) = span(a, side), span(b, side)
            for c in range(3):
                for r in range(ni):
                    at = (landing(a, side) + r) * window + landing(b, side)
                    win_ref[c, at : at + nj, :] = recvs[k][c, r * nj : (r + 1) * nj, :]
            multi_copy(k).wait_recv()

        @pl.when(exists(a, b))
        def _(k=k):
            halo_copy(k).wait_send()
            multi_copy(k).wait_send()

    @pl.loop(1, count)
    def _(o):
        row_copy(o).wait_recv()
        row_copy(o).wait_send()


    fill(source_ref, window_rows, window, False, range(all_leaves // 8))

    @pl.loop(0, all_leaves)
    def _(s):
        source_leaf(s)

    @pl.loop(0, inner_side * inner_side)
    def _(n):
        ti, tj = inner_low + n // inner_side, inner_low + lax.rem(n, inner_side)
        out_x = jnp.where(ti == inner_low, -WIDTH, WIDTH)
        out_y = jnp.where(tj == inner_low, -WIDTH, WIDTH)
        steps = [(out_x, dy) for dy in range(-WIDTH, WIDTH + 1)]
        steps += [(si - ti, out_y) for si in range(side)]
        pair_sums(ti * side + tj, ti, tj, steps, False)

    edge = own - inner_side * inner_side

    @pl.loop(0, edge)
    def _(n):
        t = jnp.where(n < side, n, jnp.where(n >= edge - side, n + own - edge, 0))
        turn = n - side
        between = (turn // 2 + 1) * side + lax.rem(turn, 2) * (side - 1)
        t = jnp.where((n >= side) & (n < edge - side), between, t)
        steps = [(dx, dy) for dx in range(-WIDTH, WIDTH + 1) for dy in range(-WIDTH, WIDTH + 1)]
        pair_sums(t, t // side, lax.rem(t, side), steps, True)

    in_window = 9 * own
    rows = block_ref[:, 0, :]
    block_lanes = -(-count // 128) * 128
    if block_lanes > count:
        rows = jnp.concatenate(
            [rows, jnp.zeros((block_lanes - count, 128), jnp.float32)], axis=0
        )
    blocks = jnp.concatenate(
        [rows[k * 128 : (k + 1) * 128].T[:MULTI] for k in range(block_lanes // 128)], axis=1
    )
    near_lane = lax.broadcasted_iota(jnp.int32, (MULTI, 128), 1)
    groups = -(-in_window // 128)
    parts = [jnp.zeros((MULTI, 128), jnp.float32) for _ in range(groups)]
    for d in range(9):
        piece = jnp.where(near_lane < own, near_ref[d], 0.0)
        at = d * own
        shift = at % 128
        if shift:
            piece = pltpu.roll(piece, shift, 1)
        parts[at // 128] = parts[at // 128] + piece
    used = in_window % 128
    if used and used + count <= 128:
        first_block = in_window
        parts[-1] = parts[-1] + pltpu.roll(blocks[:, :128], used, 1)
    else:
        first_block = groups * 128
        parts.append(blocks)
    moments = jnp.concatenate(parts, axis=1)
    total_lanes = moments.shape[1]

    lane = lax.broadcasted_iota(jnp.int32, (own, total_lanes), 1)
    row = lax.broadcasted_iota(jnp.int32, (own, total_lanes), 0)
    ti, tj = row // side, row % side
    device = lane // own
    inside = lane % own
    dx = (device // 3 - 1) * side + inside // side - ti
    dy = (device % 3 - 1) * side + inside % side - tj
    reach = jnp.maximum(jnp.abs(dx), jnp.abs(dy))
    weight = jnp.zeros((own, total_lanes), jnp.float32)
    for o, (a, b) in enumerate(CYCLE):
        column = jnp.zeros((own, total_lanes), jnp.float32)
        for t in range(own):
            kept = 1.0 - mask_ref[o, t // side, t % side].astype(jnp.float32)
            column = jnp.where(row == t, kept, column)
        weight = jnp.where((dx == a) & (dy == b), column, weight)
    weight = jnp.where(reach >= 3, 1.0, weight)
    weight = jnp.where(lane < in_window, weight, 0.0)
    number = lane - first_block
    block_x, block_y = number // leaves, number % leaves
    remote = (number >= 0) & (number < count) & (
        jnp.maximum(jnp.abs(block_x - slab), jnp.abs(block_y - leaf)) >= 2
    )
    middle = (side - 1) / 2.0
    far_x = ((block_x - slab) * side - ti).astype(jnp.float32) + middle
    far_y = ((block_y - leaf) * side - tj).astype(jnp.float32) + middle
    weight = jnp.where(remote, 1.0, weight)
    shift_x = jnp.where(remote, far_x, dx.astype(jnp.float32))
    shift_y = jnp.where(remote, far_y, dy.astype(jnp.float32))
    shift_x = jnp.where(weight == 0.0, 1.0, shift_x)
    shift_y = jnp.where(weight == 0.0, 0.0, shift_y)
    denominator = shift_x * shift_x + shift_y * shift_y
    base_x, base_y = shift_x / denominator, -shift_y / denominator
    power_x, power_y = [weight * base_x], [weight * base_y]
    for n in range(1, 2 * ORDER - 1):
        last_x, last_y = power_x[-1] * float(n), power_y[-1] * float(n)
        power_x.append(last_x * base_x - last_y * base_y)
        power_y.append(last_x * base_y + last_y * base_x)
    local_x, local_y = [], []
    moment_x = [
        moments[k : k + 1] * ((-1.0) ** (k + 1) / math.factorial(k)) for k in range(ORDER)
    ]
    moment_y = [
        moments[ORDER + k : ORDER + k + 1] * ((-1.0) ** (k + 1) / math.factorial(k))
        for k in range(ORDER)
    ]
    for m in range(ORDER):
        sum_x = jnp.zeros((own, total_lanes), jnp.float32)
        sum_y = jnp.zeros((own, total_lanes), jnp.float32)
        for k in range(ORDER):
            px, py = power_x[m + k], power_y[m + k]
            sum_x = sum_x + (moment_x[k] * px - moment_y[k] * py)
            sum_y = sum_y + (moment_x[k] * py + moment_y[k] * px)
        scale = 1.0 / math.factorial(m)
        local_x.append(jnp.sum(sum_x, axis=1, keepdims=True) * scale)
        local_y.append(jnp.sum(sum_y, axis=1, keepdims=True) * scale)

    own_x, own_y = own_ref[0], own_ref[1]
    field_x = jnp.broadcast_to(local_x[-1], own_x.shape)
    field_y = jnp.broadcast_to(local_y[-1], own_x.shape)
    for m in range(ORDER - 2, -1, -1):
        field_x, field_y = (
            field_x * own_x - field_y * own_y + local_x[m],
            field_x * own_y + field_y * own_x + local_y[m],
        )
    first = (sum_ref[2] - own_y * sum_ref[0] + field_y) * (1.0 / TWO_PI)
    second = (own_x * sum_ref[0] - sum_ref[1] + field_x) * (1.0 / TWO_PI)
    for i in range(side):
        out_ref[0, i] = first[i * side : (i + 1) * side]
        out_ref[1, i] = second[i * side : (i + 1) * side]


def body(particles, near_mask, *, slabs, leaves):
    side, count = particles.shape[1], particles.shape[3]
    own = side * side
    window = side + 2 * WIDTH
    devices = slabs * leaves
    f32 = jnp.float32
    vmem = pl.BlockSpec(memory_space=pltpu.VMEM)
    smem = pl.BlockSpec(memory_space=pltpu.SMEM)
    strips = [
        pltpu.VMEM((3, span(a, side)[1] * span(b, side)[1], count), f32) for a, b in DIRECTIONS
    ]
    bf16 = jnp.bfloat16
    return pl.pallas_call(
        functools.partial(field_kernel, slabs, leaves, side),
        out_shape=jax.ShapeDtypeStruct((2, side, side, count), f32),
        in_specs=[smem, vmem],
        out_specs=vmem,
        scratch_shapes=[
            pltpu.VMEM((3, window * window, count), f32),
            pltpu.VMEM((3, own, count), f32),
            pltpu.VMEM((9, MULTI, 128), f32),
            pltpu.VMEM((devices, 1, 128), f32),
        ] + strips + strips + [
            pltpu.VMEM((MULTI, 128), f32),
            pltpu.VMEM((1, 128), f32),
            pltpu.SemaphoreType.DMA((8,)), pltpu.SemaphoreType.DMA((8,)),
            pltpu.SemaphoreType.DMA((8,)), pltpu.SemaphoreType.DMA((8,)),
            pltpu.SemaphoreType.DMA((devices,)), pltpu.SemaphoreType.DMA((devices,)),
            pltpu.VMEM((count // 128, FEATURES * (window * window + 8), 128), f32),
            pltpu.VMEM((count // 128, FEATURES * (own + 8), 128), f32),
            pltpu.VMEM((count, FEATURES), bf16),
            pltpu.VMEM((window * window, FEATURES, count), bf16),
            pltpu.VMEM((25, 8, count), f32),
            pltpu.VMEM((3, count, 128), f32),
            pltpu.VMEM((3, own, count), f32),
        ],
        compiler_params=pltpu.CompilerParams(
            collective_id=0, has_side_effects=True, vmem_limit_bytes=48 * 1024 * 1024
        ),
        name="field",
    )(near_mask, particles)


def solution(mesh):
    return jax.shard_map(
        functools.partial(body, slabs=mesh.shape["slab"], leaves=mesh.shape["leaf"]),
        mesh=mesh,
        in_specs=(P(None, "slab", "leaf", None), P(None, "slab", "leaf")),
        out_specs=P(None, "slab", "leaf", None),
        check_vma=False,
    )
```

```python
import functools
import math

import jax
import jax.numpy as jnp
import numpy as np
from jax import lax
from jax.experimental import pallas as pl
from jax.experimental.pallas import tpu as pltpu
from jax.sharding import PartitionSpec as P

ORDER = 10
DELTA_SQUARED = 0.0025
TWO_PI = 2.0 * math.pi
MESH = pl.DeviceIdType.MESH
CYCLE = [(a, b) for a in range(-2, 3) for b in range(-2, 3) if max(abs(a), abs(b)) == 2]
DIRECTIONS = [(a, b) for a in (-1, 0, 1) for b in (-1, 0, 1) if (a, b) != (0, 0)]
WIDTH = 2
FEATURES = 48
CHUNK = 128
MULTI = 24


def span(step, side):
    return {-1: (0, WIDTH), 0: (0, side), 1: (side - WIDTH, WIDTH)}[step]


def landing(step, side):
    return {1: 0, 0: WIDTH, -1: WIDTH + side}[step]


def moment_columns(base_x, base_y, strength, lane):
    power_x, power_y = strength, jnp.zeros_like(strength)
    out = jnp.zeros(lane.shape, jnp.float32)
    for k in range(ORDER):
        if k:
            power_x, power_y = (
                power_x * base_x - power_y * base_y,
                power_x * base_y + power_y * base_x,
            )
        out = jnp.where(lane == k, jnp.sum(power_x, axis=1, keepdims=True), out)
        if k:
            out = jnp.where(lane == ORDER + k, jnp.sum(power_y, axis=1, keepdims=True), out)
    return out


def rounded(values):
    return values.astype(jnp.bfloat16).astype(jnp.float32)


def pieces(value, place, extra):
    coarse = jnp.floor(value * 32.0 + 0.5) * (1.0 / 32.0)
    rest = value - coarse
    rest_1 = rounded(rest)
    rest_2 = rounded(rest - rest_1)
    rest = rest_1 + rest_2
    coarse = coarse + place
    square = coarse * coarse
    square_1 = rounded(square)
    square_2 = square - square_1
    cross = 2.0 * coarse * rest + (rest * rest + extra)
    cross_1 = rounded(cross)
    cross_2 = rounded(cross - cross_1)
    cross_3 = cross - cross_1 - cross_2
    return dict(
        one=jnp.ones_like(value), h=coarse, l1=rest_1, l2=rest_2, s1=square_1, s2=square_2,
        c1=cross_1, c2=cross_2, c3=cross_3,
    )


HIGH = [
    ("s1", 1.0, "one"), ("s2", 1.0, "one"), ("one", 1.0, "s1"), ("one", 1.0, "s2"),
    ("h", -2.0, "h"),
]
LOW = [
    ("c1", 1.0, "one"), ("c2", 1.0, "one"), ("c3", 1.0, "one"),
    ("one", 1.0, "c1"), ("one", 1.0, "c2"), ("one", 1.0, "c3"),
    ("h", -2.0, "l1"), ("h", -2.0, "l2"), ("l1", -2.0, "h"), ("l2", -2.0, "h"),
    ("l1", -2.0, "l1"), ("l1", -2.0, "l2"), ("l2", -2.0, "l1"),
]
ROWS = [(axis, row) for rows in (HIGH, LOW) for axis in (0, 1) for row in rows]


def field_kernel(slabs, leaves, side, mask_ref, part_ref, out_ref, *refs):
    win_ref, own_ref, near_ref, block_ref = refs[:4]
    sends, recvs = refs[4:12], refs[12:20]
    multi_ref, row_ref = refs[20:22]
    halo_send, halo_recv, multi_send, multi_recv, row_send, row_recv = refs[22:28]
    source_ref, target_ref, left_ref, right_ref, gain_ref, acc_ref, sum_ref = refs[28:]
    count = slabs * leaves
    window = side + 2 * WIDTH
    own = side * side
    particles = part_ref.shape[3]
    halves = particles // 128
    all_leaves = window * window
    slab, leaf = lax.axis_index("slab"), lax.axis_index("leaf")
    me = slab * leaves + leaf

    def place(number):
        return (number // leaves, lax.rem(number, leaves))

    barrier = pltpu.get_barrier_semaphore()

    @pl.loop(1, count)
    def _(o):
        pl.semaphore_signal(
            barrier, inc=1, device_id=place(lax.rem(me + o, count)), device_id_type=MESH
        )

    for c in range(3):
        for i in range(side):
            own_ref[c, i * side : (i + 1) * side, :] = part_ref[c, i]
    win_ref[...] = jnp.zeros_like(win_ref)
    for c in range(3):
        for i in range(side):
            at = (i + WIDTH) * window + WIDTH
            win_ref[c, at : at + side, :] = part_ref[c, i]
    for k, (a, b) in enumerate(DIRECTIONS):
        (i0, ni), (j0, nj) = span(a, side), span(b, side)
        for c in range(3):
            for r in range(ni):
                sends[k][c, r * nj : (r + 1) * nj, :] = part_ref[c, i0 + r, j0 : j0 + nj, :]

    def exists(a, b):
        s, l = slab + a, leaf + b
        return (s >= 0) & (s < slabs) & (l >= 0) & (l < leaves)

    def halo_copy(k):
        a, b = DIRECTIONS[k]
        return pltpu.make_async_remote_copy(
            src_ref=sends[k], dst_ref=recvs[k],
            send_sem=halo_send.at[k], recv_sem=halo_recv.at[k],
            device_id=(slab + a, leaf + b), device_id_type=MESH,
        )

    def multi_copy(k):
        a, b = DIRECTIONS[k]
        return pltpu.make_async_remote_copy(
            src_ref=multi_ref, dst_ref=near_ref.at[(1 - a) * 3 + (1 - b)],
            send_sem=multi_send.at[k], recv_sem=multi_recv.at[k],
            device_id=(slab + a, leaf + b), device_id_type=MESH,
        )

    def row_copy(o):
        return pltpu.make_async_remote_copy(
            src_ref=row_ref, dst_ref=block_ref.at[me],
            send_sem=row_send.at[o], recv_sem=row_recv.at[o],
            device_id=place(lax.rem(me + o, count)), device_id_type=MESH,
        )

    pl.semaphore_wait(barrier, count - 1)
    for k, (a, b) in enumerate(DIRECTIONS):
        @pl.when(exists(a, b))
        def _(k=k):
            halo_copy(k).start()

    own_x, own_y, strength = own_ref[0], own_ref[1], own_ref[2]
    lane = lax.broadcasted_iota(jnp.int32, (side * side, 128), 1)
    number = lax.broadcasted_iota(jnp.int32, own_x.shape, 0)
    centred_x = (number // side).astype(jnp.float32) - (side - 1) / 2.0
    centred_y = (number % side).astype(jnp.float32) - (side - 1) / 2.0
    block = moment_columns(own_x + centred_x, own_y + centred_y, strength, lane)
    row_ref[...] = jnp.sum(block, axis=0, keepdims=True)
    block_ref[me] = row_ref[...]

    @pl.loop(1, count)
    def _(o):
        row_copy(o).start()

    columns = moment_columns(own_x, own_y, strength, lane)
    square = jnp.concatenate(
        [columns, jnp.zeros((128 - side * side, 128), jnp.float32)], axis=0
    )
    multi_ref[...] = square.T[:MULTI]
    near_ref[4] = multi_ref[...]
    for k, (a, b) in enumerate(DIRECTIONS):
        @pl.when(exists(a, b))
        def _(k=k):
            multi_copy(k).start()

        @pl.when(jnp.logical_not(exists(-a, -b)))
        def _(a=a, b=b):
            near_ref[(1 - a) * 3 + (1 - b)] = jnp.zeros((MULTI, 128), jnp.float32)

    def fill(ref, get, width, is_target, groups):
        leaf_count = width * width
        stride = leaf_count + 8
        index = lax.broadcasted_iota(jnp.int32, (8, 128), 0)
        low = 0 if is_target else WIDTH
        for g in groups:
            place_x = ((index + g * 8) // width - low).astype(jnp.float32) - (side - 1) / 2.0
            place_y = ((index + g * 8) % width - low).astype(jnp.float32) - (side - 1) / 2.0
            for half in range(halves):
                lanes = slice(half * 128, (half + 1) * 128)
                extra = DELTA_SQUARED / 2.0 if is_target else 0.0
                parts = [
                    pieces(get(c, g, lanes), place, extra)
                    for c, place in ((0, place_x), (1, place_y))
                ]
                for r in range(FEATURES):
                    if r < len(ROWS):
                        axis, (target, factor, source) = ROWS[r]
                        value = parts[axis][target] * factor if is_target else parts[axis][source]
                    else:
                        value = jnp.zeros((8, 128), jnp.float32)
                    ref[half, r * stride + g * 8 : r * stride + g * 8 + 8, :] = value


    def target_leaf(t):
        for half in range(halves):
            rows = target_ref[half, pl.ds(t, FEATURES, stride=own + 8), :]
            left_ref[half * 128 : (half + 1) * 128, :] = rows.T.astype(jnp.bfloat16)

    def source_leaf(number):
        for half in range(halves):
            lanes = slice(half * 128, (half + 1) * 128)
            rows = source_ref[half, pl.ds(number, FEATURES, stride=all_leaves + 8), :]
            right_ref[number, :, lanes] = rows.astype(jnp.bfloat16)

    def pair_sums(t, ti, tj, steps, first):
        target_leaf(t)
        sources = []
        for number, (dx, dy) in enumerate(steps):
            source = (ti + (dx + WIDTH)) * window + tj + (dy + WIDTH)
            sources.append(source)
            strength = win_ref[2, pl.ds(source, 1), :]
            if isinstance(dx, int) and isinstance(dy, int):
                if max(abs(dx), abs(dy)) == 2:
                    o = CYCLE.index((dx, dy))
                    strength = strength * mask_ref[o, ti, tj].astype(jnp.float32)
                shift_x, shift_y = float(dx), float(dy)
            else:
                dx, dy = jnp.int32(dx), jnp.int32(dy)
                o = jnp.where(dx == -2, dy + 2, jnp.where(dx == 2, dy + 13, 7 + 2 * dx))
                o = jnp.where((jnp.abs(dx) < 2) & (dy == 2), o + 1, o)
                o = jnp.maximum(0, jnp.minimum(o, len(CYCLE) - 1))
                outer = jnp.maximum(jnp.abs(dx), jnp.abs(dy)) == 2
                chosen = jnp.where(outer, mask_ref[o, ti, tj], 1)
                strength = strength * chosen.astype(jnp.float32)
                shift_x, shift_y = dx.astype(jnp.float32), dy.astype(jnp.float32)
            gain_ref[number, 0:1, :] = strength
            gain_ref[number, 1:2, :] = strength * (win_ref[0, pl.ds(source, 1), :] + shift_x)
            gain_ref[number, 2:3, :] = strength * (win_ref[1, pl.ds(source, 1), :] + shift_y)

        @pl.loop(0, particles // CHUNK)
        def _(chunk):
            at = pl.multiple_of(chunk * CHUNK, CHUNK)
            left = left_ref[pl.ds(at, CHUNK), :]
            totals = [jnp.zeros((CHUNK, 128), jnp.float32) for _ in range(3)]
            for number, source in enumerate(sources):
                distance = jnp.dot(left, right_ref[source], preferred_element_type=jnp.float32)
                inverse = pl.reciprocal(distance, approx=True)
                for half in range(halves):
                    lanes = slice(half * 128, (half + 1) * 128)
                    part = inverse[:, lanes]
                    for q in range(3):
                        totals[q] = totals[q] + part * gain_ref[number, q : q + 1, lanes]
            for q in range(3):
                acc_ref[q, pl.ds(at, CHUNK), :] = totals[q]

        for q in range(3):
            sums = jnp.concatenate(
                [
                    jnp.sum(acc_ref[q, half * 128 : (half + 1) * 128, :].T, axis=0, keepdims=True)
                    for half in range(halves)
                ],
                axis=1,
            )
            if first:
                sum_ref[q, pl.ds(t, 1), :] = sums
            else:
                sum_ref[q, pl.ds(t, 1), :] = sum_ref[q, pl.ds(t, 1), :] + sums

    def own_rows(c, g, lanes):
        return own_ref[c, g * 8 : g * 8 + 8, lanes]

    def window_rows(c, g, lanes):
        return win_ref[c, g * 8 : g * 8 + 8, lanes]

    fill(target_ref, own_rows, side, True, range(own // 8))
    fill(source_ref, window_rows, window, False, range(WIDTH, WIDTH + side))

    @pl.loop(0, own)
    def _(s):
        source_leaf((s // side + WIDTH) * window + lax.rem(s, side) + WIDTH)

    inner_side = 2 * WIDTH + 2 - side
    inner_low = side - 1 - WIDTH

    @pl.loop(0, inner_side * inner_side)
    def _(n):
        ti, tj = inner_low + n // inner_side, inner_low + lax.rem(n, inner_side)
        steps = [(si - ti, sj - tj) for si in range(side) for sj in range(side)]
        pair_sums(ti * side + tj, ti, tj, steps, True)

    for k, (a, b) in enumerate(DIRECTIONS):
        @pl.when(exists(-a, -b))
        def _(k=k, a=a, b=b):
            halo_copy(k).wait_recv()
            (i0, ni), (j0, nj) = span(a, side), span(b, side)
            for c in range(3):
                for r in range(ni):
                    at = (landing(a, side) + r) * window + landing(b, side)
                    win_ref[c, at : at + nj, :] = recvs[k][c, r * nj : (r + 1) * nj, :]
            multi_copy(k).wait_recv()

        @pl.when(exists(a, b))
        def _(k=k):
            halo_copy(k).wait_send()
            multi_copy(k).wait_send()

    @pl.loop(1, count)
    def _(o):
        row_copy(o).wait_recv()
        row_copy(o).wait_send()


    fill(source_ref, window_rows, window, False, range(all_leaves // 8))

    @pl.loop(0, all_leaves)
    def _(s):
        source_leaf(s)

    @pl.loop(0, inner_side * inner_side)
    def _(n):
        ti, tj = inner_low + n // inner_side, inner_low + lax.rem(n, inner_side)
        out_x = jnp.where(ti == inner_low, -WIDTH, WIDTH)
        out_y = jnp.where(tj == inner_low, -WIDTH, WIDTH)
        steps = [(out_x, dy) for dy in range(-WIDTH, WIDTH + 1)]
        steps += [(si - ti, out_y) for si in range(side)]
        pair_sums(ti * side + tj, ti, tj, steps, False)

    edge = own - inner_side * inner_side

    @pl.loop(0, edge)
    def _(n):
        t = jnp.where(n < side, n, jnp.where(n >= edge - side, n + own - edge, 0))
        turn = n - side
        between = (turn // 2 + 1) * side + lax.rem(turn, 2) * (side - 1)
        t = jnp.where((n >= side) & (n < edge - side), between, t)
        steps = [(dx, dy) for dx in range(-WIDTH, WIDTH + 1) for dy in range(-WIDTH, WIDTH + 1)]
        pair_sums(t, t // side, lax.rem(t, side), steps, True)

    in_window = 9 * own
    rows = block_ref[:, 0, :]
    block_lanes = -(-count // 128) * 128
    if block_lanes > count:
        rows = jnp.concatenate(
            [rows, jnp.zeros((block_lanes - count, 128), jnp.float32)], axis=0
        )
    blocks = jnp.concatenate(
        [rows[k * 128 : (k + 1) * 128].T[:MULTI] for k in range(block_lanes // 128)], axis=1
    )
    near_lane = lax.broadcasted_iota(jnp.int32, (MULTI, 128), 1)
    groups = -(-in_window // 128)
    parts = [jnp.zeros((MULTI, 128), jnp.float32) for _ in range(groups)]
    for d in range(9):
        piece = jnp.where(near_lane < own, near_ref[d], 0.0)
        at = d * own
        shift = at % 128
        if shift:
            piece = pltpu.roll(piece, shift, 1)
        parts[at // 128] = parts[at // 128] + piece
    used = in_window % 128
    if used and used + count <= 128:
        first_block = in_window
        parts[-1] = parts[-1] + pltpu.roll(blocks[:, :128], used, 1)
    else:
        first_block = groups * 128
        parts.append(blocks)
    moments = jnp.concatenate(parts, axis=1)
    total_lanes = moments.shape[1]

    lane = lax.broadcasted_iota(jnp.int32, (own, total_lanes), 1)
    row = lax.broadcasted_iota(jnp.int32, (own, total_lanes), 0)
    ti, tj = row // side, row % side
    device = lane // own
    inside = lane % own
    dx = (device // 3 - 1) * side + inside // side - ti
    dy = (device % 3 - 1) * side + inside % side - tj
    reach = jnp.maximum(jnp.abs(dx), jnp.abs(dy))
    weight = jnp.zeros((own, total_lanes), jnp.float32)
    for o, (a, b) in enumerate(CYCLE):
        column = jnp.zeros((own, total_lanes), jnp.float32)
        for t in range(own):
            kept = 1.0 - mask_ref[o, t // side, t % side].astype(jnp.float32)
            column = jnp.where(row == t, kept, column)
        weight = jnp.where((dx == a) & (dy == b), column, weight)
    weight = jnp.where(reach >= 3, 1.0, weight)
    weight = jnp.where(lane < in_window, weight, 0.0)
    number = lane - first_block
    block_x, block_y = number // leaves, number % leaves
    remote = (number >= 0) & (number < count) & (
        jnp.maximum(jnp.abs(block_x - slab), jnp.abs(block_y - leaf)) >= 2
    )
    middle = (side - 1) / 2.0
    far_x = ((block_x - slab) * side - ti).astype(jnp.float32) + middle
    far_y = ((block_y - leaf) * side - tj).astype(jnp.float32) + middle
    weight = jnp.where(remote, 1.0, weight)
    shift_x = jnp.where(remote, far_x, dx.astype(jnp.float32))
    shift_y = jnp.where(remote, far_y, dy.astype(jnp.float32))
    shift_x = jnp.where(weight == 0.0, 1.0, shift_x)
    shift_y = jnp.where(weight == 0.0, 0.0, shift_y)
    denominator = shift_x * shift_x + shift_y * shift_y
    base_x, base_y = shift_x / denominator, -shift_y / denominator
    power_x, power_y = [weight * base_x], [weight * base_y]
    for n in range(1, 2 * ORDER - 1):
        last_x, last_y = power_x[-1] * float(n), power_y[-1] * float(n)
        power_x.append(last_x * base_x - last_y * base_y)
        power_y.append(last_x * base_y + last_y * base_x)
    local_x, local_y = [], []
    moment_x = [
        moments[k : k + 1] * ((-1.0) ** (k + 1) / math.factorial(k)) for k in range(ORDER)
    ]
    moment_y = [
        moments[ORDER + k : ORDER + k + 1] * ((-1.0) ** (k + 1) / math.factorial(k))
        for k in range(ORDER)
    ]
    for m in range(ORDER):
        sum_x = jnp.zeros((own, total_lanes), jnp.float32)
        sum_y = jnp.zeros((own, total_lanes), jnp.float32)
        for k in range(ORDER):
            px, py = power_x[m + k], power_y[m + k]
            sum_x = sum_x + (moment_x[k] * px - moment_y[k] * py)
            sum_y = sum_y + (moment_x[k] * py + moment_y[k] * px)
        scale = 1.0 / math.factorial(m)
        local_x.append(jnp.sum(sum_x, axis=1, keepdims=True) * scale)
        local_y.append(jnp.sum(sum_y, axis=1, keepdims=True) * scale)

    own_x, own_y = own_ref[0], own_ref[1]
    field_x = jnp.broadcast_to(local_x[-1], own_x.shape)
    field_y = jnp.broadcast_to(local_y[-1], own_x.shape)
    for m in range(ORDER - 2, -1, -1):
        field_x, field_y = (
            field_x * own_x - field_y * own_y + local_x[m],
            field_x * own_y + field_y * own_x + local_y[m],
        )
    first = (sum_ref[2] - own_y * sum_ref[0] + field_y) * (1.0 / TWO_PI)
    second = (own_x * sum_ref[0] - sum_ref[1] + field_x) * (1.0 / TWO_PI)
    for i in range(side):
        out_ref[0, i] = first[i * side : (i + 1) * side]
        out_ref[1, i] = second[i * side : (i + 1) * side]


def body(particles, near_mask, *, slabs, leaves):
    side, count = particles.shape[1], particles.shape[3]
    own = side * side
    window = side + 2 * WIDTH
    devices = slabs * leaves
    f32 = jnp.float32
    vmem = pl.BlockSpec(memory_space=pltpu.VMEM)
    smem = pl.BlockSpec(memory_space=pltpu.SMEM)
    strips = [
        pltpu.VMEM((3, span(a, side)[1] * span(b, side)[1], count), f32) for a, b in DIRECTIONS
    ]
    bf16 = jnp.bfloat16
    return pl.pallas_call(
        functools.partial(field_kernel, slabs, leaves, side),
        out_shape=jax.ShapeDtypeStruct((2, side, side, count), f32),
        in_specs=[smem, vmem],
        out_specs=vmem,
        scratch_shapes=[
            pltpu.VMEM((3, window * window, count), f32),
            pltpu.VMEM((3, own, count), f32),
            pltpu.VMEM((9, MULTI, 128), f32),
            pltpu.VMEM((devices, 1, 128), f32),
        ] + strips + strips + [
            pltpu.VMEM((MULTI, 128), f32),
            pltpu.VMEM((1, 128), f32),
            pltpu.SemaphoreType.DMA((8,)), pltpu.SemaphoreType.DMA((8,)),
            pltpu.SemaphoreType.DMA((8,)), pltpu.SemaphoreType.DMA((8,)),
            pltpu.SemaphoreType.DMA((devices,)), pltpu.SemaphoreType.DMA((devices,)),
            pltpu.VMEM((count // 128, FEATURES * (window * window + 8), 128), f32),
            pltpu.VMEM((count // 128, FEATURES * (own + 8), 128), f32),
            pltpu.VMEM((count, FEATURES), bf16),
            pltpu.VMEM((window * window, FEATURES, count), bf16),
            pltpu.VMEM((25, 8, count), f32),
            pltpu.VMEM((3, count, 128), f32),
            pltpu.VMEM((3, own, count), f32),
        ],
        compiler_params=pltpu.CompilerParams(
            collective_id=0, has_side_effects=True, vmem_limit_bytes=48 * 1024 * 1024
        ),
        name="field",
    )(near_mask, particles)


def solution(mesh):
    return jax.shard_map(
        functools.partial(body, slabs=mesh.shape["slab"], leaves=mesh.shape["leaf"]),
        mesh=mesh,
        in_specs=(P(None, "slab", "leaf", None), P(None, "slab", "leaf")),
        out_specs=P(None, "slab", "leaf", None),
        check_vma=False,
    )
```

```python
import functools
import math

import jax
import jax.numpy as jnp
import numpy as np
from jax import lax
from jax.experimental import pallas as pl
from jax.experimental.pallas import tpu as pltpu
from jax.sharding import PartitionSpec as P

ORDER = 10
DELTA_SQUARED = 0.0025
TWO_PI = 2.0 * math.pi
MESH = pl.DeviceIdType.MESH
CYCLE = [(a, b) for a in range(-2, 3) for b in range(-2, 3) if max(abs(a), abs(b)) == 2]
DIRECTIONS = [(a, b) for a in (-1, 0, 1) for b in (-1, 0, 1) if (a, b) != (0, 0)]
WIDTH = 2
CHUNK = 64
MULTI = 24


def span(step, side):
    return {-1: (0, WIDTH), 0: (0, side), 1: (side - WIDTH, WIDTH)}[step]


def landing(step, side):
    return {1: 0, 0: WIDTH, -1: WIDTH + side}[step]


def moment_columns(base_x, base_y, strength, lane):
    power_x, power_y = strength, jnp.zeros_like(strength)
    out = jnp.zeros(lane.shape, jnp.float32)
    for k in range(ORDER):
        if k:
            power_x, power_y = (
                power_x * base_x - power_y * base_y,
                power_x * base_y + power_y * base_x,
            )
        out = jnp.where(lane == k, jnp.sum(power_x, axis=1, keepdims=True), out)
        if k:
            out = jnp.where(lane == ORDER + k, jnp.sum(power_y, axis=1, keepdims=True), out)
    return out


def field_kernel(slabs, leaves, side, mask_ref, part_ref, out_ref, *refs):
    win_ref, own_ref, near_ref, block_ref = refs[:4]
    sends, recvs = refs[4:12], refs[12:20]
    multi_ref, row_ref = refs[20:22]
    halo_send, halo_recv, multi_send, multi_recv, row_send, row_recv = refs[22:28]
    column_ref, gain_ref, acc_ref, sum_ref = refs[28:]
    count = slabs * leaves
    window = side + 2 * WIDTH
    own = side * side
    particles = part_ref.shape[3]
    halves = particles // 128
    slab, leaf = lax.axis_index("slab"), lax.axis_index("leaf")
    me = slab * leaves + leaf

    def place(number):
        return (number // leaves, lax.rem(number, leaves))

    barrier = pltpu.get_barrier_semaphore()

    @pl.loop(1, count)
    def _(o):
        pl.semaphore_signal(
            barrier, inc=1, device_id=place(lax.rem(me + o, count)), device_id_type=MESH
        )

    for c in range(3):
        for i in range(side):
            own_ref[c, i * side : (i + 1) * side, :] = part_ref[c, i]
    win_ref[...] = jnp.zeros_like(win_ref)
    for c in range(3):
        for i in range(side):
            at = (i + WIDTH) * window + WIDTH
            win_ref[c, at : at + side, :] = part_ref[c, i]
    for k, (a, b) in enumerate(DIRECTIONS):
        (i0, ni), (j0, nj) = span(a, side), span(b, side)
        for c in range(3):
            for r in range(ni):
                sends[k][c, r * nj : (r + 1) * nj, :] = part_ref[c, i0 + r, j0 : j0 + nj, :]

    def exists(a, b):
        s, l = slab + a, leaf + b
        return (s >= 0) & (s < slabs) & (l >= 0) & (l < leaves)

    def halo_copy(k):
        a, b = DIRECTIONS[k]
        return pltpu.make_async_remote_copy(
            src_ref=sends[k], dst_ref=recvs[k],
            send_sem=halo_send.at[k], recv_sem=halo_recv.at[k],
            device_id=(slab + a, leaf + b), device_id_type=MESH,
        )

    def multi_copy(k):
        a, b = DIRECTIONS[k]
        return pltpu.make_async_remote_copy(
            src_ref=multi_ref, dst_ref=near_ref.at[(1 - a) * 3 + (1 - b)],
            send_sem=multi_send.at[k], recv_sem=multi_recv.at[k],
            device_id=(slab + a, leaf + b), device_id_type=MESH,
        )

    def row_copy(o):
        return pltpu.make_async_remote_copy(
            src_ref=row_ref, dst_ref=block_ref.at[me],
            send_sem=row_send.at[o], recv_sem=row_recv.at[o],
            device_id=place(lax.rem(me + o, count)), device_id_type=MESH,
        )

    pl.semaphore_wait(barrier, count - 1)
    for k, (a, b) in enumerate(DIRECTIONS):
        @pl.when(exists(a, b))
        def _(k=k):
            halo_copy(k).start()

    own_x, own_y, strength = own_ref[0], own_ref[1], own_ref[2]
    lane = lax.broadcasted_iota(jnp.int32, (side * side, 128), 1)
    number = lax.broadcasted_iota(jnp.int32, own_x.shape, 0)
    centred_x = (number // side).astype(jnp.float32) - (side - 1) / 2.0
    centred_y = (number % side).astype(jnp.float32) - (side - 1) / 2.0
    block = moment_columns(own_x + centred_x, own_y + centred_y, strength, lane)
    row_ref[...] = jnp.sum(block, axis=0, keepdims=True)
    block_ref[me] = row_ref[...]

    @pl.loop(1, count)
    def _(o):
        row_copy(o).start()

    columns = moment_columns(own_x, own_y, strength, lane)
    square = jnp.concatenate(
        [columns, jnp.zeros((128 - side * side, 128), jnp.float32)], axis=0
    )
    multi_ref[...] = square.T[:MULTI]
    near_ref[4] = multi_ref[...]
    for k, (a, b) in enumerate(DIRECTIONS):
        @pl.when(exists(a, b))
        def _(k=k):
            multi_copy(k).start()

        @pl.when(jnp.logical_not(exists(-a, -b)))
        def _(a=a, b=b):
            near_ref[(1 - a) * 3 + (1 - b)] = jnp.zeros((MULTI, 128), jnp.float32)

    def target_leaf(t):
        for c in range(2):
            line = own_ref[c, pl.ds(t, 1), :]
            for half in range(halves):
                lanes = slice(half * 128, (half + 1) * 128)
                column_ref[c, lanes, :] = jnp.broadcast_to(line[:, lanes], (128, 128)).T

    def pair_sums(t, ti, tj, steps, first):
        target_leaf(t)
        for number, (dx, dy) in enumerate(steps):
            source = (ti + (dx + WIDTH)) * window + tj + (dy + WIDTH)
            strength = win_ref[2, pl.ds(source, 1), :]
            if isinstance(dx, int) and isinstance(dy, int):
                if max(abs(dx), abs(dy)) == 2:
                    o = CYCLE.index((dx, dy))
                    strength = strength * mask_ref[o, ti, tj].astype(jnp.float32)
                shift_x, shift_y = float(dx), float(dy)
            else:
                dx, dy = jnp.int32(dx), jnp.int32(dy)
                o = jnp.where(dx == -2, dy + 2, jnp.where(dx == 2, dy + 13, 7 + 2 * dx))
                o = jnp.where((jnp.abs(dx) < 2) & (dy == 2), o + 1, o)
                o = jnp.maximum(0, jnp.minimum(o, len(CYCLE) - 1))
                outer = jnp.maximum(jnp.abs(dx), jnp.abs(dy)) == 2
                chosen = jnp.where(outer, mask_ref[o, ti, tj], 1)
                strength = strength * chosen.astype(jnp.float32)
                shift_x, shift_y = dx.astype(jnp.float32), dy.astype(jnp.float32)
            gain_ref[number, 0:1, :] = strength
            gain_ref[number, 1:2, :] = win_ref[0, pl.ds(source, 1), :] + shift_x
            gain_ref[number, 2:3, :] = win_ref[1, pl.ds(source, 1), :] + shift_y

        @pl.loop(0, particles // CHUNK)
        def _(chunk):
            at = pl.multiple_of(chunk * CHUNK, CHUNK)
            target_x = column_ref[0, pl.ds(at, CHUNK), :]
            target_y = column_ref[1, pl.ds(at, CHUNK), :]
            total_x = jnp.zeros((CHUNK, 128), jnp.float32)
            total_y = jnp.zeros((CHUNK, 128), jnp.float32)
            for number in range(len(steps)):
                for half in range(halves):
                    lanes = slice(half * 128, (half + 1) * 128)
                    delta_x = target_x - gain_ref[number, 1:2, lanes]
                    delta_y = target_y - gain_ref[number, 2:3, lanes]
                    distance = delta_x * delta_x + (delta_y * delta_y + DELTA_SQUARED)
                    factor = gain_ref[number, 0:1, lanes] * pl.reciprocal(distance, approx=True)
                    total_x = total_x + factor * delta_x
                    total_y = total_y + factor * delta_y
            acc_ref[0, pl.ds(at, CHUNK), :] = total_x
            acc_ref[1, pl.ds(at, CHUNK), :] = total_y

        for q in range(2):
            sums = jnp.concatenate(
                [
                    jnp.sum(acc_ref[q, half * 128 : (half + 1) * 128, :].T, axis=0, keepdims=True)
                    for half in range(halves)
                ],
                axis=1,
            )
            if first:
                sum_ref[q, pl.ds(t, 1), :] = sums
            else:
                sum_ref[q, pl.ds(t, 1), :] = sum_ref[q, pl.ds(t, 1), :] + sums

    inner_side = 2 * WIDTH + 2 - side
    inner_low = side - 1 - WIDTH

    @pl.loop(0, inner_side * inner_side)
    def _(n):
        ti, tj = inner_low + n // inner_side, inner_low + lax.rem(n, inner_side)
        steps = [(si - ti, sj - tj) for si in range(side) for sj in range(side)]
        pair_sums(ti * side + tj, ti, tj, steps, True)

    for k, (a, b) in enumerate(DIRECTIONS):
        @pl.when(exists(-a, -b))
        def _(k=k, a=a, b=b):
            halo_copy(k).wait_recv()
            (i0, ni), (j0, nj) = span(a, side), span(b, side)
            for c in range(3):
                for r in range(ni):
                    at = (landing(a, side) + r) * window + landing(b, side)
                    win_ref[c, at : at + nj, :] = recvs[k][c, r * nj : (r + 1) * nj, :]
            multi_copy(k).wait_recv()

        @pl.when(exists(a, b))
        def _(k=k):
            halo_copy(k).wait_send()
            multi_copy(k).wait_send()

    @pl.loop(1, count)
    def _(o):
        row_copy(o).wait_recv()
        row_copy(o).wait_send()


    @pl.loop(0, inner_side * inner_side)
    def _(n):
        ti, tj = inner_low + n // inner_side, inner_low + lax.rem(n, inner_side)
        out_x = jnp.where(ti == inner_low, -WIDTH, WIDTH)
        out_y = jnp.where(tj == inner_low, -WIDTH, WIDTH)
        steps = [(out_x, dy) for dy in range(-WIDTH, WIDTH + 1)]
        steps += [(si - ti, out_y) for si in range(side)]
        pair_sums(ti * side + tj, ti, tj, steps, False)

    edge = own - inner_side * inner_side

    @pl.loop(0, edge)
    def _(n):
        t = jnp.where(n < side, n, jnp.where(n >= edge - side, n + own - edge, 0))
        turn = n - side
        between = (turn // 2 + 1) * side + lax.rem(turn, 2) * (side - 1)
        t = jnp.where((n >= side) & (n < edge - side), between, t)
        steps = [(dx, dy) for dx in range(-WIDTH, WIDTH + 1) for dy in range(-WIDTH, WIDTH + 1)]
        pair_sums(t, t // side, lax.rem(t, side), steps, True)

    in_window = 9 * own
    rows = block_ref[:, 0, :]
    block_lanes = -(-count // 128) * 128
    if block_lanes > count:
        rows = jnp.concatenate(
            [rows, jnp.zeros((block_lanes - count, 128), jnp.float32)], axis=0
        )
    blocks = jnp.concatenate(
        [rows[k * 128 : (k + 1) * 128].T[:MULTI] for k in range(block_lanes // 128)], axis=1
    )
    near_lane = lax.broadcasted_iota(jnp.int32, (MULTI, 128), 1)
    groups = -(-in_window // 128)
    parts = [jnp.zeros((MULTI, 128), jnp.float32) for _ in range(groups)]
    for d in range(9):
        piece = jnp.where(near_lane < own, near_ref[d], 0.0)
        at = d * own
        shift = at % 128
        if shift:
            piece = pltpu.roll(piece, shift, 1)
        parts[at // 128] = parts[at // 128] + piece
    used = in_window % 128
    if used and used + count <= 128:
        first_block = in_window
        parts[-1] = parts[-1] + pltpu.roll(blocks[:, :128], used, 1)
    else:
        first_block = groups * 128
        parts.append(blocks)
    moments = jnp.concatenate(parts, axis=1)
    total_lanes = moments.shape[1]

    lane = lax.broadcasted_iota(jnp.int32, (own, total_lanes), 1)
    row = lax.broadcasted_iota(jnp.int32, (own, total_lanes), 0)
    ti, tj = row // side, row % side
    device = lane // own
    inside = lane % own
    dx = (device // 3 - 1) * side + inside // side - ti
    dy = (device % 3 - 1) * side + inside % side - tj
    reach = jnp.maximum(jnp.abs(dx), jnp.abs(dy))
    weight = jnp.zeros((own, total_lanes), jnp.float32)
    for o, (a, b) in enumerate(CYCLE):
        column = jnp.zeros((own, total_lanes), jnp.float32)
        for t in range(own):
            kept = 1.0 - mask_ref[o, t // side, t % side].astype(jnp.float32)
            column = jnp.where(row == t, kept, column)
        weight = jnp.where((dx == a) & (dy == b), column, weight)
    weight = jnp.where(reach >= 3, 1.0, weight)
    weight = jnp.where(lane < in_window, weight, 0.0)
    number = lane - first_block
    block_x, block_y = number // leaves, number % leaves
    remote = (number >= 0) & (number < count) & (
        jnp.maximum(jnp.abs(block_x - slab), jnp.abs(block_y - leaf)) >= 2
    )
    middle = (side - 1) / 2.0
    far_x = ((block_x - slab) * side - ti).astype(jnp.float32) + middle
    far_y = ((block_y - leaf) * side - tj).astype(jnp.float32) + middle
    weight = jnp.where(remote, 1.0, weight)
    shift_x = jnp.where(remote, far_x, dx.astype(jnp.float32))
    shift_y = jnp.where(remote, far_y, dy.astype(jnp.float32))
    shift_x = jnp.where(weight == 0.0, 1.0, shift_x)
    shift_y = jnp.where(weight == 0.0, 0.0, shift_y)
    denominator = shift_x * shift_x + shift_y * shift_y
    base_x, base_y = shift_x / denominator, -shift_y / denominator
    power_x, power_y = [weight * base_x], [weight * base_y]
    for n in range(1, 2 * ORDER - 1):
        last_x, last_y = power_x[-1] * float(n), power_y[-1] * float(n)
        power_x.append(last_x * base_x - last_y * base_y)
        power_y.append(last_x * base_y + last_y * base_x)
    local_x, local_y = [], []
    moment_x = [
        moments[k : k + 1] * ((-1.0) ** (k + 1) / math.factorial(k)) for k in range(ORDER)
    ]
    moment_y = [
        moments[ORDER + k : ORDER + k + 1] * ((-1.0) ** (k + 1) / math.factorial(k))
        for k in range(ORDER)
    ]
    for m in range(ORDER):
        sum_x = jnp.zeros((own, total_lanes), jnp.float32)
        sum_y = jnp.zeros((own, total_lanes), jnp.float32)
        for k in range(ORDER):
            px, py = power_x[m + k], power_y[m + k]
            sum_x = sum_x + (moment_x[k] * px - moment_y[k] * py)
            sum_y = sum_y + (moment_x[k] * py + moment_y[k] * px)
        scale = 1.0 / math.factorial(m)
        local_x.append(jnp.sum(sum_x, axis=1, keepdims=True) * scale)
        local_y.append(jnp.sum(sum_y, axis=1, keepdims=True) * scale)

    own_x, own_y = own_ref[0], own_ref[1]
    field_x = jnp.broadcast_to(local_x[-1], own_x.shape)
    field_y = jnp.broadcast_to(local_y[-1], own_x.shape)
    for m in range(ORDER - 2, -1, -1):
        field_x, field_y = (
            field_x * own_x - field_y * own_y + local_x[m],
            field_x * own_y + field_y * own_x + local_y[m],
        )
    first = (field_y - sum_ref[1]) * (1.0 / TWO_PI)
    second = (field_x + sum_ref[0]) * (1.0 / TWO_PI)
    for i in range(side):
        out_ref[0, i] = first[i * side : (i + 1) * side]
        out_ref[1, i] = second[i * side : (i + 1) * side]


def body(particles, near_mask, *, slabs, leaves):
    side, count = particles.shape[1], particles.shape[3]
    own = side * side
    window = side + 2 * WIDTH
    devices = slabs * leaves
    f32 = jnp.float32
    vmem = pl.BlockSpec(memory_space=pltpu.VMEM)
    smem = pl.BlockSpec(memory_space=pltpu.SMEM)
    strips = [
        pltpu.VMEM((3, span(a, side)[1] * span(b, side)[1], count), f32) for a, b in DIRECTIONS
    ]
    return pl.pallas_call(
        functools.partial(field_kernel, slabs, leaves, side),
        out_shape=jax.ShapeDtypeStruct((2, side, side, count), f32),
        in_specs=[smem, vmem],
        out_specs=vmem,
        scratch_shapes=[
            pltpu.VMEM((3, window * window, count), f32),
            pltpu.VMEM((3, own, count), f32),
            pltpu.VMEM((9, MULTI, 128), f32),
            pltpu.VMEM((devices, 1, 128), f32),
        ] + strips + strips + [
            pltpu.VMEM((MULTI, 128), f32),
            pltpu.VMEM((1, 128), f32),
            pltpu.SemaphoreType.DMA((8,)), pltpu.SemaphoreType.DMA((8,)),
            pltpu.SemaphoreType.DMA((8,)), pltpu.SemaphoreType.DMA((8,)),
            pltpu.SemaphoreType.DMA((devices,)), pltpu.SemaphoreType.DMA((devices,)),
            pltpu.VMEM((2, count, 128), f32),
            pltpu.VMEM((25, 8, count), f32),
            pltpu.VMEM((2, count, 128), f32),
            pltpu.VMEM((2, own, count), f32),
        ],
        compiler_params=pltpu.CompilerParams(
            collective_id=0, has_side_effects=True, vmem_limit_bytes=48 * 1024 * 1024
        ),
        name="field",
    )(near_mask, particles)


def solution(mesh):
    return jax.shard_map(
        functools.partial(body, slabs=mesh.shape["slab"], leaves=mesh.shape["leaf"]),
        mesh=mesh,
        in_specs=(P(None, "slab", "leaf", None), P(None, "slab", "leaf")),
        out_specs=P(None, "slab", "leaf", None),
        check_vma=False,
    )
```

```python
import functools
import math

import jax
import jax.numpy as jnp
import numpy as np
from jax import lax
from jax.experimental import pallas as pl
from jax.experimental.pallas import tpu as pltpu
from jax.sharding import PartitionSpec as P

ORDER = 10
DELTA_SQUARED = 0.0025
TWO_PI = 2.0 * math.pi
MESH = pl.DeviceIdType.MESH
CYCLE = [(a, b) for a in range(-2, 3) for b in range(-2, 3) if max(abs(a), abs(b)) == 2]
DIRECTIONS = [(a, b) for a in (-1, 0, 1) for b in (-1, 0, 1) if (a, b) != (0, 0)]
WIDTH = 2
FEATURES = 48
CHUNK = 128
MULTI = 24


def span(step, side):
    return {-1: (0, WIDTH), 0: (0, side), 1: (side - WIDTH, WIDTH)}[step]


def landing(step, side):
    return {1: 0, 0: WIDTH, -1: WIDTH + side}[step]


def moment_columns(base_x, base_y, strength, lane):
    power_x, power_y = strength, jnp.zeros_like(strength)
    out = jnp.zeros(lane.shape, jnp.float32)
    for k in range(ORDER):
        if k:
            power_x, power_y = (
                power_x * base_x - power_y * base_y,
                power_x * base_y + power_y * base_x,
            )
        out = jnp.where(lane == k, jnp.sum(power_x, axis=1, keepdims=True), out)
        if k:
            out = jnp.where(lane == ORDER + k, jnp.sum(power_y, axis=1, keepdims=True), out)
    return out


def rounded(values):
    return values.astype(jnp.bfloat16).astype(jnp.float32)


def pieces(value, place, extra):
    coarse = jnp.floor(value * 32.0 + 0.5) * (1.0 / 32.0)
    rest = value - coarse
    rest_1 = rounded(rest)
    rest_2 = rounded(rest - rest_1)
    rest = rest_1 + rest_2
    coarse = coarse + place
    square = coarse * coarse
    square_1 = rounded(square)
    square_2 = square - square_1
    cross = 2.0 * coarse * rest + (rest * rest + extra)
    cross_1 = rounded(cross)
    cross_2 = rounded(cross - cross_1)
    cross_3 = cross - cross_1 - cross_2
    return dict(
        one=jnp.ones_like(value), h=coarse, l1=rest_1, l2=rest_2, s1=square_1, s2=square_2,
        c1=cross_1, c2=cross_2, c3=cross_3,
    )


HIGH = [
    ("s1", 1.0, "one"), ("s2", 1.0, "one"), ("one", 1.0, "s1"), ("one", 1.0, "s2"),
    ("h", -2.0, "h"),
]
LOW = [
    ("c1", 1.0, "one"), ("c2", 1.0, "one"), ("c3", 1.0, "one"),
    ("one", 1.0, "c1"), ("one", 1.0, "c2"), ("one", 1.0, "c3"),
    ("h", -2.0, "l1"), ("h", -2.0, "l2"), ("l1", -2.0, "h"), ("l2", -2.0, "h"),
    ("l1", -2.0, "l1"), ("l1", -2.0, "l2"), ("l2", -2.0, "l1"),
]
ROWS = [(axis, row) for rows in (HIGH, LOW) for axis in (0, 1) for row in rows]


def reciprocals(values):
    out = []
    for first in range(0, len(values) - 1, 2):
        a, b = values[first : first + 2]
        both_inverse = pl.reciprocal(a * b, approx=True)
        out += [both_inverse * b, both_inverse * a]
    if len(values) % 2:
        out.append(pl.reciprocal(values[-1], approx=True))
    return out


def field_kernel(slabs, leaves, side, mask_ref, part_ref, out_ref, *refs):
    win_ref, own_ref, near_ref, block_ref = refs[:4]
    sends, recvs = refs[4:12], refs[12:20]
    multi_ref, row_ref = refs[20:22]
    halo_send, halo_recv, multi_send, multi_recv, row_send, row_recv = refs[22:28]
    source_ref, target_ref, left_ref, right_ref, gain_ref, acc_ref, sum_ref = refs[28:]
    count = slabs * leaves
    window = side + 2 * WIDTH
    own = side * side
    particles = part_ref.shape[3]
    halves = particles // 128
    all_leaves = window * window
    slab, leaf = lax.axis_index("slab"), lax.axis_index("leaf")
    me = slab * leaves + leaf

    def place(number):
        return (number // leaves, lax.rem(number, leaves))

    barrier = pltpu.get_barrier_semaphore()

    @pl.loop(1, count)
    def _(o):
        pl.semaphore_signal(
            barrier, inc=1, device_id=place(lax.rem(me + o, count)), device_id_type=MESH
        )

    for c in range(3):
        for i in range(side):
            own_ref[c, i * side : (i + 1) * side, :] = part_ref[c, i]
    win_ref[...] = jnp.zeros_like(win_ref)
    for c in range(3):
        for i in range(side):
            at = (i + WIDTH) * window + WIDTH
            win_ref[c, at : at + side, :] = part_ref[c, i]
    for k, (a, b) in enumerate(DIRECTIONS):
        (i0, ni), (j0, nj) = span(a, side), span(b, side)
        for c in range(3):
            for r in range(ni):
                sends[k][c, r * nj : (r + 1) * nj, :] = part_ref[c, i0 + r, j0 : j0 + nj, :]

    def exists(a, b):
        s, l = slab + a, leaf + b
        return (s >= 0) & (s < slabs) & (l >= 0) & (l < leaves)

    def halo_copy(k):
        a, b = DIRECTIONS[k]
        return pltpu.make_async_remote_copy(
            src_ref=sends[k], dst_ref=recvs[k],
            send_sem=halo_send.at[k], recv_sem=halo_recv.at[k],
            device_id=(slab + a, leaf + b), device_id_type=MESH,
        )

    def multi_copy(k):
        a, b = DIRECTIONS[k]
        return pltpu.make_async_remote_copy(
            src_ref=multi_ref, dst_ref=near_ref.at[(1 - a) * 3 + (1 - b)],
            send_sem=multi_send.at[k], recv_sem=multi_recv.at[k],
            device_id=(slab + a, leaf + b), device_id_type=MESH,
        )

    def row_copy(o):
        return pltpu.make_async_remote_copy(
            src_ref=row_ref, dst_ref=block_ref.at[me],
            send_sem=row_send.at[o], recv_sem=row_recv.at[o],
            device_id=place(lax.rem(me + o, count)), device_id_type=MESH,
        )

    pl.semaphore_wait(barrier, count - 1)
    for k, (a, b) in enumerate(DIRECTIONS):
        @pl.when(exists(a, b))
        def _(k=k):
            halo_copy(k).start()

    own_x, own_y, strength = own_ref[0], own_ref[1], own_ref[2]
    lane = lax.broadcasted_iota(jnp.int32, (side * side, 128), 1)
    number = lax.broadcasted_iota(jnp.int32, own_x.shape, 0)
    centred_x = (number // side).astype(jnp.float32) - (side - 1) / 2.0
    centred_y = (number % side).astype(jnp.float32) - (side - 1) / 2.0
    block = moment_columns(own_x + centred_x, own_y + centred_y, strength, lane)
    row_ref[...] = jnp.sum(block, axis=0, keepdims=True)
    block_ref[me] = row_ref[...]

    @pl.loop(1, count)
    def _(o):
        row_copy(o).start()

    columns = moment_columns(own_x, own_y, strength, lane)
    square = jnp.concatenate(
        [columns, jnp.zeros((128 - side * side, 128), jnp.float32)], axis=0
    )
    multi_ref[...] = square.T[:MULTI]
    near_ref[4] = multi_ref[...]
    for k, (a, b) in enumerate(DIRECTIONS):
        @pl.when(exists(a, b))
        def _(k=k):
            multi_copy(k).start()

        @pl.when(jnp.logical_not(exists(-a, -b)))
        def _(a=a, b=b):
            near_ref[(1 - a) * 3 + (1 - b)] = jnp.zeros((MULTI, 128), jnp.float32)

    def fill(ref, get, width, is_target, groups):
        leaf_count = width * width
        stride = leaf_count + 8
        index = lax.broadcasted_iota(jnp.int32, (8, 128), 0)
        low = 0 if is_target else WIDTH
        for g in groups:
            place_x = ((index + g * 8) // width - low).astype(jnp.float32) - (side - 1) / 2.0
            place_y = ((index + g * 8) % width - low).astype(jnp.float32) - (side - 1) / 2.0
            for half in range(halves):
                lanes = slice(half * 128, (half + 1) * 128)
                extra = DELTA_SQUARED / 2.0 if is_target else 0.0
                parts = [
                    pieces(get(c, g, lanes), place, extra)
                    for c, place in ((0, place_x), (1, place_y))
                ]
                for r in range(FEATURES):
                    if r < len(ROWS):
                        axis, (target, factor, source) = ROWS[r]
                        value = parts[axis][target] * factor if is_target else parts[axis][source]
                    else:
                        value = jnp.zeros((8, 128), jnp.float32)
                    ref[half, r * stride + g * 8 : r * stride + g * 8 + 8, :] = value


    def target_leaf(t):
        for half in range(halves):
            rows = target_ref[half, pl.ds(t, FEATURES, stride=own + 8), :]
            left_ref[half * 128 : (half + 1) * 128, :] = rows.T.astype(jnp.bfloat16)

    def source_leaf(number):
        for half in range(halves):
            lanes = slice(half * 128, (half + 1) * 128)
            rows = source_ref[half, pl.ds(number, FEATURES, stride=all_leaves + 8), :]
            right_ref[number, :, lanes] = rows.astype(jnp.bfloat16)

    def pair_sums(t, ti, tj, steps, first):
        target_leaf(t)
        sources = []
        for number, (dx, dy) in enumerate(steps):
            source = (ti + (dx + WIDTH)) * window + tj + (dy + WIDTH)
            sources.append(source)
            strength = win_ref[2, pl.ds(source, 1), :]
            if isinstance(dx, int) and isinstance(dy, int):
                if max(abs(dx), abs(dy)) == 2:
                    o = CYCLE.index((dx, dy))
                    strength = strength * mask_ref[o, ti, tj].astype(jnp.float32)
                shift_x, shift_y = float(dx), float(dy)
            else:
                dx, dy = jnp.int32(dx), jnp.int32(dy)
                o = jnp.where(dx == -2, dy + 2, jnp.where(dx == 2, dy + 13, 7 + 2 * dx))
                o = jnp.where((jnp.abs(dx) < 2) & (dy == 2), o + 1, o)
                o = jnp.maximum(0, jnp.minimum(o, len(CYCLE) - 1))
                outer = jnp.maximum(jnp.abs(dx), jnp.abs(dy)) == 2
                chosen = jnp.where(outer, mask_ref[o, ti, tj], 1)
                strength = strength * chosen.astype(jnp.float32)
                shift_x, shift_y = dx.astype(jnp.float32), dy.astype(jnp.float32)
            gain_ref[number, 0:1, :] = strength
            gain_ref[number, 1:2, :] = strength * (win_ref[0, pl.ds(source, 1), :] + shift_x)
            gain_ref[number, 2:3, :] = strength * (win_ref[1, pl.ds(source, 1), :] + shift_y)

        @pl.loop(0, particles // CHUNK)
        def _(chunk):
            at = pl.multiple_of(chunk * CHUNK, CHUNK)
            left = left_ref[pl.ds(at, CHUNK), :]
            totals = [jnp.zeros((CHUNK, 128), jnp.float32) for _ in range(3)]
            for number, source in enumerate(sources):
                distance = jnp.dot(left, right_ref[source], preferred_element_type=jnp.float32)
                inverses = reciprocals(
                    [distance[:, half * 128 : (half + 1) * 128] for half in range(halves)]
                )
                for half in range(halves):
                    lanes = slice(half * 128, (half + 1) * 128)
                    for q in range(3):
                        totals[q] = totals[q] + inverses[half] * gain_ref[number, q : q + 1, lanes]
            for q in range(3):
                acc_ref[q, pl.ds(at, CHUNK), :] = totals[q]

        for q in range(3):
            sums = jnp.concatenate(
                [
                    jnp.sum(acc_ref[q, half * 128 : (half + 1) * 128, :].T, axis=0, keepdims=True)
                    for half in range(halves)
                ],
                axis=1,
            )
            if first:
                sum_ref[q, pl.ds(t, 1), :] = sums
            else:
                sum_ref[q, pl.ds(t, 1), :] = sum_ref[q, pl.ds(t, 1), :] + sums

    def own_rows(c, g, lanes):
        return own_ref[c, g * 8 : g * 8 + 8, lanes]

    def window_rows(c, g, lanes):
        return win_ref[c, g * 8 : g * 8 + 8, lanes]

    fill(target_ref, own_rows, side, True, range(own // 8))
    fill(source_ref, window_rows, window, False, range(WIDTH, WIDTH + side))

    @pl.loop(0, own)
    def _(s):
        source_leaf((s // side + WIDTH) * window + lax.rem(s, side) + WIDTH)

    inner_side = 2 * WIDTH + 2 - side
    inner_low = side - 1 - WIDTH

    @pl.loop(0, inner_side * inner_side)
    def _(n):
        ti, tj = inner_low + n // inner_side, inner_low + lax.rem(n, inner_side)
        steps = [(si - ti, sj - tj) for si in range(side) for sj in range(side)]
        pair_sums(ti * side + tj, ti, tj, steps, True)

    for k, (a, b) in enumerate(DIRECTIONS):
        @pl.when(exists(-a, -b))
        def _(k=k, a=a, b=b):
            halo_copy(k).wait_recv()
            (i0, ni), (j0, nj) = span(a, side), span(b, side)
            for c in range(3):
                for r in range(ni):
                    at = (landing(a, side) + r) * window + landing(b, side)
                    win_ref[c, at : at + nj, :] = recvs[k][c, r * nj : (r + 1) * nj, :]
            multi_copy(k).wait_recv()

        @pl.when(exists(a, b))
        def _(k=k):
            halo_copy(k).wait_send()
            multi_copy(k).wait_send()

    @pl.loop(1, count)
    def _(o):
        row_copy(o).wait_recv()
        row_copy(o).wait_send()


    fill(source_ref, window_rows, window, False, range(all_leaves // 8))

    @pl.loop(0, all_leaves)
    def _(s):
        source_leaf(s)

    @pl.loop(0, inner_side * inner_side)
    def _(n):
        ti, tj = inner_low + n // inner_side, inner_low + lax.rem(n, inner_side)
        out_x = jnp.where(ti == inner_low, -WIDTH, WIDTH)
        out_y = jnp.where(tj == inner_low, -WIDTH, WIDTH)
        steps = [(out_x, dy) for dy in range(-WIDTH, WIDTH + 1)]
        steps += [(si - ti, out_y) for si in range(side)]
        pair_sums(ti * side + tj, ti, tj, steps, False)

    edge = own - inner_side * inner_side

    @pl.loop(0, edge)
    def _(n):
        t = jnp.where(n < side, n, jnp.where(n >= edge - side, n + own - edge, 0))
        turn = n - side
        between = (turn // 2 + 1) * side + lax.rem(turn, 2) * (side - 1)
        t = jnp.where((n >= side) & (n < edge - side), between, t)
        steps = [(dx, dy) for dx in range(-WIDTH, WIDTH + 1) for dy in range(-WIDTH, WIDTH + 1)]
        pair_sums(t, t // side, lax.rem(t, side), steps, True)

    in_window = 9 * own
    rows = block_ref[:, 0, :]
    block_lanes = -(-count // 128) * 128
    if block_lanes > count:
        rows = jnp.concatenate(
            [rows, jnp.zeros((block_lanes - count, 128), jnp.float32)], axis=0
        )
    blocks = jnp.concatenate(
        [rows[k * 128 : (k + 1) * 128].T[:MULTI] for k in range(block_lanes // 128)], axis=1
    )
    near_lane = lax.broadcasted_iota(jnp.int32, (MULTI, 128), 1)
    groups = -(-in_window // 128)
    parts = [jnp.zeros((MULTI, 128), jnp.float32) for _ in range(groups)]
    for d in range(9):
        piece = jnp.where(near_lane < own, near_ref[d], 0.0)
        at = d * own
        shift = at % 128
        if shift:
            piece = pltpu.roll(piece, shift, 1)
        parts[at // 128] = parts[at // 128] + piece
    used = in_window % 128
    if used and used + count <= 128:
        first_block = in_window
        parts[-1] = parts[-1] + pltpu.roll(blocks[:, :128], used, 1)
    else:
        first_block = groups * 128
        parts.append(blocks)
    moments = jnp.concatenate(parts, axis=1)
    total_lanes = moments.shape[1]

    lane = lax.broadcasted_iota(jnp.int32, (own, total_lanes), 1)
    row = lax.broadcasted_iota(jnp.int32, (own, total_lanes), 0)
    ti, tj = row // side, row % side
    device = lane // own
    inside = lane % own
    dx = (device // 3 - 1) * side + inside // side - ti
    dy = (device % 3 - 1) * side + inside % side - tj
    reach = jnp.maximum(jnp.abs(dx), jnp.abs(dy))
    weight = jnp.zeros((own, total_lanes), jnp.float32)
    for o, (a, b) in enumerate(CYCLE):
        column = jnp.zeros((own, total_lanes), jnp.float32)
        for t in range(own):
            kept = 1.0 - mask_ref[o, t // side, t % side].astype(jnp.float32)
            column = jnp.where(row == t, kept, column)
        weight = jnp.where((dx == a) & (dy == b), column, weight)
    weight = jnp.where(reach >= 3, 1.0, weight)
    weight = jnp.where(lane < in_window, weight, 0.0)
    number = lane - first_block
    block_x, block_y = number // leaves, number % leaves
    remote = (number >= 0) & (number < count) & (
        jnp.maximum(jnp.abs(block_x - slab), jnp.abs(block_y - leaf)) >= 2
    )
    middle = (side - 1) / 2.0
    far_x = ((block_x - slab) * side - ti).astype(jnp.float32) + middle
    far_y = ((block_y - leaf) * side - tj).astype(jnp.float32) + middle
    weight = jnp.where(remote, 1.0, weight)
    shift_x = jnp.where(remote, far_x, dx.astype(jnp.float32))
    shift_y = jnp.where(remote, far_y, dy.astype(jnp.float32))
    shift_x = jnp.where(weight == 0.0, 1.0, shift_x)
    shift_y = jnp.where(weight == 0.0, 0.0, shift_y)
    denominator = shift_x * shift_x + shift_y * shift_y
    base_x, base_y = shift_x / denominator, -shift_y / denominator
    power_x, power_y = [weight * base_x], [weight * base_y]
    for n in range(1, 2 * ORDER - 1):
        last_x, last_y = power_x[-1] * float(n), power_y[-1] * float(n)
        power_x.append(last_x * base_x - last_y * base_y)
        power_y.append(last_x * base_y + last_y * base_x)
    local_x, local_y = [], []
    moment_x = [
        moments[k : k + 1] * ((-1.0) ** (k + 1) / math.factorial(k)) for k in range(ORDER)
    ]
    moment_y = [
        moments[ORDER + k : ORDER + k + 1] * ((-1.0) ** (k + 1) / math.factorial(k))
        for k in range(ORDER)
    ]
    for m in range(ORDER):
        sum_x = jnp.zeros((own, total_lanes), jnp.float32)
        sum_y = jnp.zeros((own, total_lanes), jnp.float32)
        for k in range(ORDER):
            px, py = power_x[m + k], power_y[m + k]
            sum_x = sum_x + (moment_x[k] * px - moment_y[k] * py)
            sum_y = sum_y + (moment_x[k] * py + moment_y[k] * px)
        scale = 1.0 / math.factorial(m)
        local_x.append(jnp.sum(sum_x, axis=1, keepdims=True) * scale)
        local_y.append(jnp.sum(sum_y, axis=1, keepdims=True) * scale)

    own_x, own_y = own_ref[0], own_ref[1]
    field_x = jnp.broadcast_to(local_x[-1], own_x.shape)
    field_y = jnp.broadcast_to(local_y[-1], own_x.shape)
    for m in range(ORDER - 2, -1, -1):
        field_x, field_y = (
            field_x * own_x - field_y * own_y + local_x[m],
            field_x * own_y + field_y * own_x + local_y[m],
        )
    first = (sum_ref[2] - own_y * sum_ref[0] + field_y) * (1.0 / TWO_PI)
    second = (own_x * sum_ref[0] - sum_ref[1] + field_x) * (1.0 / TWO_PI)
    for i in range(side):
        out_ref[0, i] = first[i * side : (i + 1) * side]
        out_ref[1, i] = second[i * side : (i + 1) * side]


def body(particles, near_mask, *, slabs, leaves):
    side, count = particles.shape[1], particles.shape[3]
    own = side * side
    window = side + 2 * WIDTH
    devices = slabs * leaves
    f32 = jnp.float32
    vmem = pl.BlockSpec(memory_space=pltpu.VMEM)
    smem = pl.BlockSpec(memory_space=pltpu.SMEM)
    strips = [
        pltpu.VMEM((3, span(a, side)[1] * span(b, side)[1], count), f32) for a, b in DIRECTIONS
    ]
    bf16 = jnp.bfloat16
    return pl.pallas_call(
        functools.partial(field_kernel, slabs, leaves, side),
        out_shape=jax.ShapeDtypeStruct((2, side, side, count), f32),
        in_specs=[smem, vmem],
        out_specs=vmem,
        scratch_shapes=[
            pltpu.VMEM((3, window * window, count), f32),
            pltpu.VMEM((3, own, count), f32),
            pltpu.VMEM((9, MULTI, 128), f32),
            pltpu.VMEM((devices, 1, 128), f32),
        ] + strips + strips + [
            pltpu.VMEM((MULTI, 128), f32),
            pltpu.VMEM((1, 128), f32),
            pltpu.SemaphoreType.DMA((8,)), pltpu.SemaphoreType.DMA((8,)),
            pltpu.SemaphoreType.DMA((8,)), pltpu.SemaphoreType.DMA((8,)),
            pltpu.SemaphoreType.DMA((devices,)), pltpu.SemaphoreType.DMA((devices,)),
            pltpu.VMEM((count // 128, FEATURES * (window * window + 8), 128), f32),
            pltpu.VMEM((count // 128, FEATURES * (own + 8), 128), f32),
            pltpu.VMEM((count, FEATURES), bf16),
            pltpu.VMEM((window * window, FEATURES, count), bf16),
            pltpu.VMEM((25, 8, count), f32),
            pltpu.VMEM((3, count, 128), f32),
            pltpu.VMEM((3, own, count), f32),
        ],
        compiler_params=pltpu.CompilerParams(
            collective_id=0, has_side_effects=True, vmem_limit_bytes=48 * 1024 * 1024
        ),
        name="field",
    )(near_mask, particles)


def solution(mesh):
    return jax.shard_map(
        functools.partial(body, slabs=mesh.shape["slab"], leaves=mesh.shape["leaf"]),
        mesh=mesh,
        in_specs=(P(None, "slab", "leaf", None), P(None, "slab", "leaf")),
        out_specs=P(None, "slab", "leaf", None),
        check_vma=False,
    )
```

```python
import functools
import math

import jax
import jax.numpy as jnp
import numpy as np
from jax import lax
from jax.experimental import pallas as pl
from jax.experimental.pallas import tpu as pltpu
from jax.sharding import PartitionSpec as P

ORDER = 10
DELTA_SQUARED = 0.0025
TWO_PI = 2.0 * math.pi
MESH = pl.DeviceIdType.MESH
CYCLE = [(a, b) for a in range(-2, 3) for b in range(-2, 3) if max(abs(a), abs(b)) == 2]
DIRECTIONS = [(a, b) for a in (-1, 0, 1) for b in (-1, 0, 1) if (a, b) != (0, 0)]
WIDTH = 2
FEATURES = 48
CHUNK = 128
MULTI = 24


def span(step, side):
    return {-1: (0, WIDTH), 0: (0, side), 1: (side - WIDTH, WIDTH)}[step]


def landing(step, side):
    return {1: 0, 0: WIDTH, -1: WIDTH + side}[step]


def moment_columns(base_x, base_y, strength, lane):
    power_x, power_y = strength, jnp.zeros_like(strength)
    out = jnp.zeros(lane.shape, jnp.float32)
    for k in range(ORDER):
        if k:
            power_x, power_y = (
                power_x * base_x - power_y * base_y,
                power_x * base_y + power_y * base_x,
            )
        out = jnp.where(lane == k, jnp.sum(power_x, axis=1, keepdims=True), out)
        if k:
            out = jnp.where(lane == ORDER + k, jnp.sum(power_y, axis=1, keepdims=True), out)
    return out


def rounded(values):
    return values.astype(jnp.bfloat16).astype(jnp.float32)


def pieces(value, place, extra):
    coarse = jnp.floor(value * 32.0 + 0.5) * (1.0 / 32.0)
    rest = value - coarse
    rest_1 = rounded(rest)
    rest_2 = rounded(rest - rest_1)
    rest = rest_1 + rest_2
    coarse = coarse + place
    square = coarse * coarse
    square_1 = rounded(square)
    square_2 = square - square_1
    cross = 2.0 * coarse * rest + (rest * rest + extra)
    cross_1 = rounded(cross)
    cross_2 = rounded(cross - cross_1)
    cross_3 = cross - cross_1 - cross_2
    return dict(
        one=jnp.ones_like(value), h=coarse, l1=rest_1, l2=rest_2, s1=square_1, s2=square_2,
        c1=cross_1, c2=cross_2, c3=cross_3,
    )


HIGH = [
    ("s1", 1.0, "one"), ("s2", 1.0, "one"), ("one", 1.0, "s1"), ("one", 1.0, "s2"),
    ("h", -2.0, "h"),
]
LOW = [
    ("c1", 1.0, "one"), ("c2", 1.0, "one"), ("c3", 1.0, "one"),
    ("one", 1.0, "c1"), ("one", 1.0, "c2"), ("one", 1.0, "c3"),
    ("h", -2.0, "l1"), ("h", -2.0, "l2"), ("l1", -2.0, "h"), ("l2", -2.0, "h"),
    ("l1", -2.0, "l1"), ("l1", -2.0, "l2"), ("l2", -2.0, "l1"),
]
ROWS = [(axis, row) for rows in (HIGH, LOW) for axis in (0, 1) for row in rows]


def reciprocals(values):
    out = []
    for first in range(0, len(values) - 1, 2):
        a, b = values[first : first + 2]
        both_inverse = pl.reciprocal(a * b, approx=True)
        out += [both_inverse * b, both_inverse * a]
    if len(values) % 2:
        out.append(pl.reciprocal(values[-1], approx=True))
    return out


def field_kernel(slabs, leaves, side, mask_ref, part_ref, out_ref, *refs):
    win_ref, own_ref, near_ref, block_ref = refs[:4]
    sends, recvs = refs[4:12], refs[12:20]
    multi_ref, row_ref = refs[20:22]
    halo_send, halo_recv, multi_send, multi_recv, row_send, row_recv = refs[22:28]
    source_ref, target_ref, left_ref, right_ref, gain_ref, sum_ref = refs[28:]
    count = slabs * leaves
    window = side + 2 * WIDTH
    own = side * side
    particles = part_ref.shape[3]
    halves = particles // 128
    all_leaves = window * window
    slab, leaf = lax.axis_index("slab"), lax.axis_index("leaf")
    me = slab * leaves + leaf

    def place(number):
        return (number // leaves, lax.rem(number, leaves))

    barrier = pltpu.get_barrier_semaphore()

    @pl.loop(1, count)
    def _(o):
        pl.semaphore_signal(
            barrier, inc=1, device_id=place(lax.rem(me + o, count)), device_id_type=MESH
        )

    for c in range(3):
        for i in range(side):
            own_ref[c, i * side : (i + 1) * side, :] = part_ref[c, i]
    win_ref[...] = jnp.zeros_like(win_ref)
    for c in range(3):
        for i in range(side):
            at = (i + WIDTH) * window + WIDTH
            win_ref[c, at : at + side, :] = part_ref[c, i]
    for k, (a, b) in enumerate(DIRECTIONS):
        (i0, ni), (j0, nj) = span(a, side), span(b, side)
        for c in range(3):
            for r in range(ni):
                sends[k][c, r * nj : (r + 1) * nj, :] = part_ref[c, i0 + r, j0 : j0 + nj, :]

    def exists(a, b):
        s, l = slab + a, leaf + b
        return (s >= 0) & (s < slabs) & (l >= 0) & (l < leaves)

    def halo_copy(k):
        a, b = DIRECTIONS[k]
        return pltpu.make_async_remote_copy(
            src_ref=sends[k], dst_ref=recvs[k],
            send_sem=halo_send.at[k], recv_sem=halo_recv.at[k],
            device_id=(slab + a, leaf + b), device_id_type=MESH,
        )

    def multi_copy(k):
        a, b = DIRECTIONS[k]
        return pltpu.make_async_remote_copy(
            src_ref=multi_ref, dst_ref=near_ref.at[(1 - a) * 3 + (1 - b)],
            send_sem=multi_send.at[k], recv_sem=multi_recv.at[k],
            device_id=(slab + a, leaf + b), device_id_type=MESH,
        )

    def row_copy(o):
        return pltpu.make_async_remote_copy(
            src_ref=row_ref, dst_ref=block_ref.at[me],
            send_sem=row_send.at[o], recv_sem=row_recv.at[o],
            device_id=place(lax.rem(me + o, count)), device_id_type=MESH,
        )

    pl.semaphore_wait(barrier, count - 1)
    for k, (a, b) in enumerate(DIRECTIONS):
        @pl.when(exists(a, b))
        def _(k=k):
            halo_copy(k).start()

    own_x, own_y, strength = own_ref[0], own_ref[1], own_ref[2]
    lane = lax.broadcasted_iota(jnp.int32, (side * side, 128), 1)
    number = lax.broadcasted_iota(jnp.int32, own_x.shape, 0)
    centred_x = (number // side).astype(jnp.float32) - (side - 1) / 2.0
    centred_y = (number % side).astype(jnp.float32) - (side - 1) / 2.0
    block = moment_columns(own_x + centred_x, own_y + centred_y, strength, lane)
    row_ref[...] = jnp.sum(block, axis=0, keepdims=True)
    block_ref[me] = row_ref[...]

    @pl.loop(1, count)
    def _(o):
        row_copy(o).start()

    columns = moment_columns(own_x, own_y, strength, lane)
    square = jnp.concatenate(
        [columns, jnp.zeros((128 - side * side, 128), jnp.float32)], axis=0
    )
    multi_ref[...] = square.T[:MULTI]
    near_ref[4] = multi_ref[...]
    for k, (a, b) in enumerate(DIRECTIONS):
        @pl.when(exists(a, b))
        def _(k=k):
            multi_copy(k).start()

        @pl.when(jnp.logical_not(exists(-a, -b)))
        def _(a=a, b=b):
            near_ref[(1 - a) * 3 + (1 - b)] = jnp.zeros((MULTI, 128), jnp.float32)

    def fill(ref, get, width, is_target, groups):
        leaf_count = width * width
        stride = leaf_count + 8
        index = lax.broadcasted_iota(jnp.int32, (8, 128), 0)
        low = 0 if is_target else WIDTH
        for g in groups:
            place_x = ((index + g * 8) // width - low).astype(jnp.float32) - (side - 1) / 2.0
            place_y = ((index + g * 8) % width - low).astype(jnp.float32) - (side - 1) / 2.0
            for half in range(halves):
                lanes = slice(half * 128, (half + 1) * 128)
                extra = DELTA_SQUARED / 2.0 if is_target else 0.0
                parts = [
                    pieces(get(c, g, lanes), place, extra)
                    for c, place in ((0, place_x), (1, place_y))
                ]
                for r in range(FEATURES):
                    if r < len(ROWS):
                        axis, (target, factor, source) = ROWS[r]
                        value = parts[axis][target] * factor if is_target else parts[axis][source]
                    else:
                        value = jnp.zeros((8, 128), jnp.float32)
                    ref[half, r * stride + g * 8 : r * stride + g * 8 + 8, :] = value


    def target_leaf(t):
        for half in range(halves):
            rows = target_ref[half, pl.ds(t, FEATURES, stride=own + 8), :]
            left_ref[half * 128 : (half + 1) * 128, :] = rows.T.astype(jnp.bfloat16)

    def source_leaf(number):
        for half in range(halves):
            lanes = slice(half * 128, (half + 1) * 128)
            rows = source_ref[half, pl.ds(number, FEATURES, stride=all_leaves + 8), :]
            right_ref[number, :, lanes] = rows.astype(jnp.bfloat16)

    def pair_sums(t, ti, tj, steps, first):
        target_leaf(t)
        sources = []
        for number, (dx, dy) in enumerate(steps):
            source = (ti + (dx + WIDTH)) * window + tj + (dy + WIDTH)
            sources.append(source)
            strength = win_ref[2, pl.ds(source, 1), :]
            if isinstance(dx, int) and isinstance(dy, int):
                if max(abs(dx), abs(dy)) == 2:
                    o = CYCLE.index((dx, dy))
                    strength = strength * mask_ref[o, ti, tj].astype(jnp.float32)
                shift_x, shift_y = float(dx), float(dy)
            else:
                dx, dy = jnp.int32(dx), jnp.int32(dy)
                o = jnp.where(dx == -2, dy + 2, jnp.where(dx == 2, dy + 13, 7 + 2 * dx))
                o = jnp.where((jnp.abs(dx) < 2) & (dy == 2), o + 1, o)
                o = jnp.maximum(0, jnp.minimum(o, len(CYCLE) - 1))
                outer = jnp.maximum(jnp.abs(dx), jnp.abs(dy)) == 2
                chosen = jnp.where(outer, mask_ref[o, ti, tj], 1)
                strength = strength * chosen.astype(jnp.float32)
                shift_x, shift_y = dx.astype(jnp.float32), dy.astype(jnp.float32)
            gain_ref[number, 0:1, :] = strength
            gain_ref[number, 1:2, :] = strength * (win_ref[0, pl.ds(source, 1), :] + shift_x)
            gain_ref[number, 2:3, :] = strength * (win_ref[1, pl.ds(source, 1), :] + shift_y)

        lines = [[] for _ in range(3)]
        for at in range(0, particles, CHUNK):
            left = left_ref[at : at + CHUNK, :]
            totals = [jnp.zeros((CHUNK, 128), jnp.float32) for _ in range(3)]
            for number, source in enumerate(sources):
                distance = jnp.dot(left, right_ref[source], preferred_element_type=jnp.float32)
                inverses = reciprocals(
                    [distance[:, half * 128 : (half + 1) * 128] for half in range(halves)]
                )
                for half in range(halves):
                    lanes = slice(half * 128, (half + 1) * 128)
                    for q in range(3):
                        totals[q] = totals[q] + inverses[half] * gain_ref[number, q : q + 1, lanes]
            for q in range(3):
                lines[q].append(jnp.sum(totals[q].T, axis=0, keepdims=True))

        for q in range(3):
            sums = jnp.concatenate(lines[q], axis=1)
            if first:
                sum_ref[q, pl.ds(t, 1), :] = sums
            else:
                sum_ref[q, pl.ds(t, 1), :] = sum_ref[q, pl.ds(t, 1), :] + sums

    def own_rows(c, g, lanes):
        return own_ref[c, g * 8 : g * 8 + 8, lanes]

    def window_rows(c, g, lanes):
        return win_ref[c, g * 8 : g * 8 + 8, lanes]

    fill(target_ref, own_rows, side, True, range(own // 8))
    fill(source_ref, window_rows, window, False, range(WIDTH, WIDTH + side))

    @pl.loop(0, own)
    def _(s):
        source_leaf((s // side + WIDTH) * window + lax.rem(s, side) + WIDTH)

    inner_side = 2 * WIDTH + 2 - side
    inner_low = side - 1 - WIDTH

    @pl.loop(0, inner_side * inner_side)
    def _(n):
        ti, tj = inner_low + n // inner_side, inner_low + lax.rem(n, inner_side)
        steps = [(si - ti, sj - tj) for si in range(side) for sj in range(side)]
        pair_sums(ti * side + tj, ti, tj, steps, True)

    for k, (a, b) in enumerate(DIRECTIONS):
        @pl.when(exists(-a, -b))
        def _(k=k, a=a, b=b):
            halo_copy(k).wait_recv()
            (i0, ni), (j0, nj) = span(a, side), span(b, side)
            for c in range(3):
                for r in range(ni):
                    at = (landing(a, side) + r) * window + landing(b, side)
                    win_ref[c, at : at + nj, :] = recvs[k][c, r * nj : (r + 1) * nj, :]
            multi_copy(k).wait_recv()

        @pl.when(exists(a, b))
        def _(k=k):
            halo_copy(k).wait_send()
            multi_copy(k).wait_send()

    @pl.loop(1, count)
    def _(o):
        row_copy(o).wait_recv()
        row_copy(o).wait_send()


    fill(source_ref, window_rows, window, False, range(all_leaves // 8))

    @pl.loop(0, all_leaves)
    def _(s):
        source_leaf(s)

    @pl.loop(0, inner_side * inner_side)
    def _(n):
        ti, tj = inner_low + n // inner_side, inner_low + lax.rem(n, inner_side)
        out_x = jnp.where(ti == inner_low, -WIDTH, WIDTH)
        out_y = jnp.where(tj == inner_low, -WIDTH, WIDTH)
        steps = [(out_x, dy) for dy in range(-WIDTH, WIDTH + 1)]
        steps += [(si - ti, out_y) for si in range(side)]
        pair_sums(ti * side + tj, ti, tj, steps, False)

    edge = own - inner_side * inner_side

    @pl.loop(0, edge)
    def _(n):
        t = jnp.where(n < side, n, jnp.where(n >= edge - side, n + own - edge, 0))
        turn = n - side
        between = (turn // 2 + 1) * side + lax.rem(turn, 2) * (side - 1)
        t = jnp.where((n >= side) & (n < edge - side), between, t)
        steps = [(dx, dy) for dx in range(-WIDTH, WIDTH + 1) for dy in range(-WIDTH, WIDTH + 1)]
        pair_sums(t, t // side, lax.rem(t, side), steps, True)

    in_window = 9 * own
    rows = block_ref[:, 0, :]
    block_lanes = -(-count // 128) * 128
    if block_lanes > count:
        rows = jnp.concatenate(
            [rows, jnp.zeros((block_lanes - count, 128), jnp.float32)], axis=0
        )
    blocks = jnp.concatenate(
        [rows[k * 128 : (k + 1) * 128].T[:MULTI] for k in range(block_lanes // 128)], axis=1
    )
    near_lane = lax.broadcasted_iota(jnp.int32, (MULTI, 128), 1)
    groups = -(-in_window // 128)
    parts = [jnp.zeros((MULTI, 128), jnp.float32) for _ in range(groups)]
    for d in range(9):
        piece = jnp.where(near_lane < own, near_ref[d], 0.0)
        at = d * own
        shift = at % 128
        if shift:
            piece = pltpu.roll(piece, shift, 1)
        parts[at // 128] = parts[at // 128] + piece
    used = in_window % 128
    if used and used + count <= 128:
        first_block = in_window
        parts[-1] = parts[-1] + pltpu.roll(blocks[:, :128], used, 1)
    else:
        first_block = groups * 128
        parts.append(blocks)
    moments = jnp.concatenate(parts, axis=1)
    total_lanes = moments.shape[1]

    lane = lax.broadcasted_iota(jnp.int32, (own, total_lanes), 1)
    row = lax.broadcasted_iota(jnp.int32, (own, total_lanes), 0)
    ti, tj = row // side, row % side
    device = lane // own
    inside = lane % own
    dx = (device // 3 - 1) * side + inside // side - ti
    dy = (device % 3 - 1) * side + inside % side - tj
    reach = jnp.maximum(jnp.abs(dx), jnp.abs(dy))
    weight = jnp.zeros((own, total_lanes), jnp.float32)
    for o, (a, b) in enumerate(CYCLE):
        column = jnp.zeros((own, total_lanes), jnp.float32)
        for t in range(own):
            kept = 1.0 - mask_ref[o, t // side, t % side].astype(jnp.float32)
            column = jnp.where(row == t, kept, column)
        weight = jnp.where((dx == a) & (dy == b), column, weight)
    weight = jnp.where(reach >= 3, 1.0, weight)
    weight = jnp.where(lane < in_window, weight, 0.0)
    number = lane - first_block
    block_x, block_y = number // leaves, number % leaves
    remote = (number >= 0) & (number < count) & (
        jnp.maximum(jnp.abs(block_x - slab), jnp.abs(block_y - leaf)) >= 2
    )
    middle = (side - 1) / 2.0
    far_x = ((block_x - slab) * side - ti).astype(jnp.float32) + middle
    far_y = ((block_y - leaf) * side - tj).astype(jnp.float32) + middle
    weight = jnp.where(remote, 1.0, weight)
    shift_x = jnp.where(remote, far_x, dx.astype(jnp.float32))
    shift_y = jnp.where(remote, far_y, dy.astype(jnp.float32))
    shift_x = jnp.where(weight == 0.0, 1.0, shift_x)
    shift_y = jnp.where(weight == 0.0, 0.0, shift_y)
    denominator = shift_x * shift_x + shift_y * shift_y
    base_x, base_y = shift_x / denominator, -shift_y / denominator
    power_x, power_y = [weight * base_x], [weight * base_y]
    for n in range(1, 2 * ORDER - 1):
        last_x, last_y = power_x[-1] * float(n), power_y[-1] * float(n)
        power_x.append(last_x * base_x - last_y * base_y)
        power_y.append(last_x * base_y + last_y * base_x)
    local_x, local_y = [], []
    moment_x = [
        moments[k : k + 1] * ((-1.0) ** (k + 1) / math.factorial(k)) for k in range(ORDER)
    ]
    moment_y = [
        moments[ORDER + k : ORDER + k + 1] * ((-1.0) ** (k + 1) / math.factorial(k))
        for k in range(ORDER)
    ]
    for m in range(ORDER):
        sum_x = jnp.zeros((own, total_lanes), jnp.float32)
        sum_y = jnp.zeros((own, total_lanes), jnp.float32)
        for k in range(ORDER):
            px, py = power_x[m + k], power_y[m + k]
            sum_x = sum_x + (moment_x[k] * px - moment_y[k] * py)
            sum_y = sum_y + (moment_x[k] * py + moment_y[k] * px)
        scale = 1.0 / math.factorial(m)
        local_x.append(jnp.sum(sum_x, axis=1, keepdims=True) * scale)
        local_y.append(jnp.sum(sum_y, axis=1, keepdims=True) * scale)

    own_x, own_y = own_ref[0], own_ref[1]
    field_x = jnp.broadcast_to(local_x[-1], own_x.shape)
    field_y = jnp.broadcast_to(local_y[-1], own_x.shape)
    for m in range(ORDER - 2, -1, -1):
        field_x, field_y = (
            field_x * own_x - field_y * own_y + local_x[m],
            field_x * own_y + field_y * own_x + local_y[m],
        )
    first = (sum_ref[2] - own_y * sum_ref[0] + field_y) * (1.0 / TWO_PI)
    second = (own_x * sum_ref[0] - sum_ref[1] + field_x) * (1.0 / TWO_PI)
    for i in range(side):
        out_ref[0, i] = first[i * side : (i + 1) * side]
        out_ref[1, i] = second[i * side : (i + 1) * side]


def body(particles, near_mask, *, slabs, leaves):
    side, count = particles.shape[1], particles.shape[3]
    own = side * side
    window = side + 2 * WIDTH
    devices = slabs * leaves
    f32 = jnp.float32
    vmem = pl.BlockSpec(memory_space=pltpu.VMEM)
    smem = pl.BlockSpec(memory_space=pltpu.SMEM)
    strips = [
        pltpu.VMEM((3, span(a, side)[1] * span(b, side)[1], count), f32) for a, b in DIRECTIONS
    ]
    bf16 = jnp.bfloat16
    return pl.pallas_call(
        functools.partial(field_kernel, slabs, leaves, side),
        out_shape=jax.ShapeDtypeStruct((2, side, side, count), f32),
        in_specs=[smem, vmem],
        out_specs=vmem,
        scratch_shapes=[
            pltpu.VMEM((3, window * window, count), f32),
            pltpu.VMEM((3, own, count), f32),
            pltpu.VMEM((9, MULTI, 128), f32),
            pltpu.VMEM((devices, 1, 128), f32),
        ] + strips + strips + [
            pltpu.VMEM((MULTI, 128), f32),
            pltpu.VMEM((1, 128), f32),
            pltpu.SemaphoreType.DMA((8,)), pltpu.SemaphoreType.DMA((8,)),
            pltpu.SemaphoreType.DMA((8,)), pltpu.SemaphoreType.DMA((8,)),
            pltpu.SemaphoreType.DMA((devices,)), pltpu.SemaphoreType.DMA((devices,)),
            pltpu.VMEM((count // 128, FEATURES * (window * window + 8), 128), f32),
            pltpu.VMEM((count // 128, FEATURES * (own + 8), 128), f32),
            pltpu.VMEM((count, FEATURES), bf16),
            pltpu.VMEM((window * window, FEATURES, count), bf16),
            pltpu.VMEM((25, 8, count), f32),
            pltpu.VMEM((3, own, count), f32),
        ],
        compiler_params=pltpu.CompilerParams(
            collective_id=0, has_side_effects=True, vmem_limit_bytes=48 * 1024 * 1024
        ),
        name="field",
    )(near_mask, particles)


def solution(mesh):
    return jax.shard_map(
        functools.partial(body, slabs=mesh.shape["slab"], leaves=mesh.shape["leaf"]),
        mesh=mesh,
        in_specs=(P(None, "slab", "leaf", None), P(None, "slab", "leaf")),
        out_specs=P(None, "slab", "leaf", None),
        check_vma=False,
    )
```

```python
import functools
import math

import jax
import jax.numpy as jnp
import numpy as np
from jax import lax
from jax.experimental import pallas as pl
from jax.experimental.pallas import tpu as pltpu
from jax.sharding import PartitionSpec as P

ORDER = 10
DELTA_SQUARED = 0.0025
TWO_PI = 2.0 * math.pi
MESH = pl.DeviceIdType.MESH
CYCLE = [(a, b) for a in range(-2, 3) for b in range(-2, 3) if max(abs(a), abs(b)) == 2]
DIRECTIONS = [(a, b) for a in (-1, 0, 1) for b in (-1, 0, 1) if (a, b) != (0, 0)]
WIDTH = 2
FEATURES = 48
CHUNK = 128
MULTI = 24


def span(step, side):
    return {-1: (0, WIDTH), 0: (0, side), 1: (side - WIDTH, WIDTH)}[step]


def landing(step, side):
    return {1: 0, 0: WIDTH, -1: WIDTH + side}[step]


def moment_columns(base_x, base_y, strength, lane):
    power_x, power_y = strength, jnp.zeros_like(strength)
    out = jnp.zeros(lane.shape, jnp.float32)
    for k in range(ORDER):
        if k:
            power_x, power_y = (
                power_x * base_x - power_y * base_y,
                power_x * base_y + power_y * base_x,
            )
        out = jnp.where(lane == k, jnp.sum(power_x, axis=1, keepdims=True), out)
        if k:
            out = jnp.where(lane == ORDER + k, jnp.sum(power_y, axis=1, keepdims=True), out)
    return out


def rounded(values):
    return values.astype(jnp.bfloat16).astype(jnp.float32)


def pieces(value, place, extra):
    coarse = jnp.floor(value * 32.0 + 0.5) * (1.0 / 32.0)
    rest = value - coarse
    rest_1 = rounded(rest)
    rest_2 = rounded(rest - rest_1)
    rest = rest_1 + rest_2
    coarse = coarse + place
    square = coarse * coarse
    square_1 = rounded(square)
    square_2 = square - square_1
    cross = 2.0 * coarse * rest + (rest * rest + extra)
    cross_1 = rounded(cross)
    cross_2 = rounded(cross - cross_1)
    cross_3 = cross - cross_1 - cross_2
    return dict(
        one=jnp.ones_like(value), h=coarse, l1=rest_1, l2=rest_2, s1=square_1, s2=square_2,
        c1=cross_1, c2=cross_2, c3=cross_3,
    )


HIGH = [
    ("s1", 1.0, "one"), ("s2", 1.0, "one"), ("one", 1.0, "s1"), ("one", 1.0, "s2"),
    ("h", -2.0, "h"),
]
LOW = [
    ("c1", 1.0, "one"), ("c2", 1.0, "one"), ("c3", 1.0, "one"),
    ("one", 1.0, "c1"), ("one", 1.0, "c2"), ("one", 1.0, "c3"),
    ("h", -2.0, "l1"), ("h", -2.0, "l2"), ("l1", -2.0, "h"), ("l2", -2.0, "h"),
    ("l1", -2.0, "l1"), ("l1", -2.0, "l2"), ("l2", -2.0, "l1"),
]
ROWS = [(axis, row) for rows in (HIGH, LOW) for axis in (0, 1) for row in rows]


def reciprocals(values):
    out = []
    for first in range(0, len(values) - 1, 2):
        a, b = values[first : first + 2]
        both_inverse = pl.reciprocal(a * b, approx=True)
        out += [both_inverse * b, both_inverse * a]
    if len(values) % 2:
        out.append(pl.reciprocal(values[-1], approx=True))
    return out


def field_kernel(slabs, leaves, side, mask_ref, part_ref, out_ref, *refs):
    win_ref, own_ref, near_ref, block_ref = refs[:4]
    sends, recvs = refs[4:12], refs[12:20]
    multi_ref, row_ref = refs[20:22]
    halo_send, halo_recv, multi_send, multi_recv, row_send, row_recv = refs[22:28]
    source_ref, target_ref, left_ref, right_ref, gain_ref, sum_ref = refs[28:]
    count = slabs * leaves
    window = side + 2 * WIDTH
    own = side * side
    particles = part_ref.shape[3]
    halves = particles // 128
    all_leaves = window * window
    slab, leaf = lax.axis_index("slab"), lax.axis_index("leaf")
    me = slab * leaves + leaf

    def place(number):
        return (number // leaves, lax.rem(number, leaves))

    barrier = pltpu.get_barrier_semaphore()

    @pl.loop(1, count)
    def _(o):
        pl.semaphore_signal(
            barrier, inc=1, device_id=place(lax.rem(me + o, count)), device_id_type=MESH
        )

    for c in range(3):
        for i in range(side):
            own_ref[c, i * side : (i + 1) * side, :] = part_ref[c, i]
    win_ref[...] = jnp.zeros_like(win_ref)
    for c in range(3):
        for i in range(side):
            at = (i + WIDTH) * window + WIDTH
            win_ref[c, at : at + side, :] = part_ref[c, i]
    for k, (a, b) in enumerate(DIRECTIONS):
        (i0, ni), (j0, nj) = span(a, side), span(b, side)
        for c in range(3):
            for r in range(ni):
                sends[k][c, r * nj : (r + 1) * nj, :] = part_ref[c, i0 + r, j0 : j0 + nj, :]

    def exists(a, b):
        s, l = slab + a, leaf + b
        return (s >= 0) & (s < slabs) & (l >= 0) & (l < leaves)

    def halo_copy(k):
        a, b = DIRECTIONS[k]
        return pltpu.make_async_remote_copy(
            src_ref=sends[k], dst_ref=recvs[k],
            send_sem=halo_send.at[k], recv_sem=halo_recv.at[k],
            device_id=(slab + a, leaf + b), device_id_type=MESH,
        )

    def multi_copy(k):
        a, b = DIRECTIONS[k]
        return pltpu.make_async_remote_copy(
            src_ref=multi_ref, dst_ref=near_ref.at[(1 - a) * 3 + (1 - b)],
            send_sem=multi_send.at[k], recv_sem=multi_recv.at[k],
            device_id=(slab + a, leaf + b), device_id_type=MESH,
        )

    def row_copy(o):
        return pltpu.make_async_remote_copy(
            src_ref=row_ref, dst_ref=block_ref.at[me],
            send_sem=row_send.at[o], recv_sem=row_recv.at[o],
            device_id=place(lax.rem(me + o, count)), device_id_type=MESH,
        )

    pl.semaphore_wait(barrier, count - 1)
    for k, (a, b) in enumerate(DIRECTIONS):
        @pl.when(exists(a, b))
        def _(k=k):
            halo_copy(k).start()

    own_x, own_y, strength = own_ref[0], own_ref[1], own_ref[2]
    lane = lax.broadcasted_iota(jnp.int32, (side * side, 128), 1)
    number = lax.broadcasted_iota(jnp.int32, own_x.shape, 0)
    centred_x = (number // side).astype(jnp.float32) - (side - 1) / 2.0
    centred_y = (number % side).astype(jnp.float32) - (side - 1) / 2.0
    block = moment_columns(own_x + centred_x, own_y + centred_y, strength, lane)
    row_ref[...] = jnp.sum(block, axis=0, keepdims=True)
    block_ref[me] = row_ref[...]

    @pl.loop(1, count)
    def _(o):
        row_copy(o).start()

    columns = moment_columns(own_x, own_y, strength, lane)
    square = jnp.concatenate(
        [columns, jnp.zeros((128 - side * side, 128), jnp.float32)], axis=0
    )
    multi_ref[...] = square.T[:MULTI]
    near_ref[4] = multi_ref[...]
    for k, (a, b) in enumerate(DIRECTIONS):
        @pl.when(exists(a, b))
        def _(k=k):
            multi_copy(k).start()

        @pl.when(jnp.logical_not(exists(-a, -b)))
        def _(a=a, b=b):
            near_ref[(1 - a) * 3 + (1 - b)] = jnp.zeros((MULTI, 128), jnp.float32)

    def fill(ref, get, width, is_target, groups):
        leaf_count = width * width
        stride = leaf_count + 8
        index = lax.broadcasted_iota(jnp.int32, (8, 128), 0)
        low = 0 if is_target else WIDTH
        for g in groups:
            place_x = ((index + g * 8) // width - low).astype(jnp.float32) - (side - 1) / 2.0
            place_y = ((index + g * 8) % width - low).astype(jnp.float32) - (side - 1) / 2.0
            for half in range(halves):
                lanes = slice(half * 128, (half + 1) * 128)
                extra = DELTA_SQUARED / 2.0 if is_target else 0.0
                parts = [
                    pieces(get(c, g, lanes), place, extra)
                    for c, place in ((0, place_x), (1, place_y))
                ]
                for r in range(FEATURES):
                    if r < len(ROWS):
                        axis, (target, factor, source) = ROWS[r]
                        value = parts[axis][target] * factor if is_target else parts[axis][source]
                    else:
                        value = jnp.zeros((8, 128), jnp.float32)
                    ref[half, r * stride + g * 8 : r * stride + g * 8 + 8, :] = value


    def target_leaf(t):
        for half in range(halves):
            rows = target_ref[half, pl.ds(t, FEATURES, stride=own + 8), :]
            left_ref[half * 128 : (half + 1) * 128, :] = rows.T.astype(jnp.bfloat16)

    def source_leaf(number):
        for half in range(halves):
            lanes = slice(half * 128, (half + 1) * 128)
            rows = source_ref[half, pl.ds(number, FEATURES, stride=all_leaves + 8), :]
            right_ref[number, :, lanes] = rows.astype(jnp.bfloat16)

    def pair_sums(t, ti, tj, steps, first):
        target_leaf(t)
        sources = []
        for number, (dx, dy) in enumerate(steps):
            source = (ti + (dx + WIDTH)) * window + tj + (dy + WIDTH)
            sources.append(source)
            strength = win_ref[2, pl.ds(source, 1), :]
            if isinstance(dx, int) and isinstance(dy, int):
                if max(abs(dx), abs(dy)) == 2:
                    o = CYCLE.index((dx, dy))
                    strength = strength * mask_ref[o, ti, tj].astype(jnp.float32)
                shift_x, shift_y = float(dx), float(dy)
            else:
                dx, dy = jnp.int32(dx), jnp.int32(dy)
                o = jnp.where(dx == -2, dy + 2, jnp.where(dx == 2, dy + 13, 7 + 2 * dx))
                o = jnp.where((jnp.abs(dx) < 2) & (dy == 2), o + 1, o)
                o = jnp.maximum(0, jnp.minimum(o, len(CYCLE) - 1))
                outer = jnp.maximum(jnp.abs(dx), jnp.abs(dy)) == 2
                chosen = jnp.where(outer, mask_ref[o, ti, tj], 1)
                strength = strength * chosen.astype(jnp.float32)
                shift_x, shift_y = dx.astype(jnp.float32), dy.astype(jnp.float32)
            gain_ref[number, 0:1, :] = strength
            gain_ref[number, 1:2, :] = strength * (win_ref[0, pl.ds(source, 1), :] + shift_x)
            gain_ref[number, 2:3, :] = strength * (win_ref[1, pl.ds(source, 1), :] + shift_y)

        lines = [[] for _ in range(3)]
        for at in range(0, particles, CHUNK):
            left = left_ref[at : at + CHUNK, :]
            totals = [jnp.zeros((CHUNK, 128), jnp.float32) for _ in range(3)]
            for number, source in enumerate(sources):
                distance = jnp.dot(left, right_ref[source], preferred_element_type=jnp.float32)
                inverses = reciprocals(
                    [distance[:, half * 128 : (half + 1) * 128] for half in range(halves)]
                )
                for half in range(halves):
                    lanes = slice(half * 128, (half + 1) * 128)
                    for q in range(3):
                        totals[q] = totals[q] + inverses[half] * gain_ref[number, q : q + 1, lanes]
            for q in range(3):
                lines[q].append(jnp.sum(totals[q].T, axis=0, keepdims=True))

        for q in range(3):
            sums = jnp.concatenate(lines[q], axis=1)
            if first:
                sum_ref[q, pl.ds(t, 1), :] = sums
            else:
                sum_ref[q, pl.ds(t, 1), :] = sum_ref[q, pl.ds(t, 1), :] + sums

    def own_rows(c, g, lanes):
        return own_ref[c, g * 8 : g * 8 + 8, lanes]

    def window_rows(c, g, lanes):
        return win_ref[c, g * 8 : g * 8 + 8, lanes]

    fill(target_ref, own_rows, side, True, range(own // 8))
    fill(source_ref, window_rows, window, False, range(WIDTH, WIDTH + side))

    @pl.loop(0, own, unroll=8)
    def _(s):
        source_leaf((s // side + WIDTH) * window + lax.rem(s, side) + WIDTH)

    inner_side = 2 * WIDTH + 2 - side
    inner_low = side - 1 - WIDTH

    @pl.loop(0, inner_side * inner_side)
    def _(n):
        ti, tj = inner_low + n // inner_side, inner_low + lax.rem(n, inner_side)
        steps = [(si - ti, sj - tj) for si in range(side) for sj in range(side)]
        pair_sums(ti * side + tj, ti, tj, steps, True)

    for k, (a, b) in enumerate(DIRECTIONS):
        @pl.when(exists(-a, -b))
        def _(k=k, a=a, b=b):
            halo_copy(k).wait_recv()
            (i0, ni), (j0, nj) = span(a, side), span(b, side)
            for c in range(3):
                for r in range(ni):
                    at = (landing(a, side) + r) * window + landing(b, side)
                    win_ref[c, at : at + nj, :] = recvs[k][c, r * nj : (r + 1) * nj, :]
            multi_copy(k).wait_recv()

        @pl.when(exists(a, b))
        def _(k=k):
            halo_copy(k).wait_send()
            multi_copy(k).wait_send()

    @pl.loop(1, count)
    def _(o):
        row_copy(o).wait_recv()
        row_copy(o).wait_send()


    fill(source_ref, window_rows, window, False, range(all_leaves // 8))

    @pl.loop(0, all_leaves, unroll=8)
    def _(s):
        source_leaf(s)

    @pl.loop(0, inner_side * inner_side)
    def _(n):
        ti, tj = inner_low + n // inner_side, inner_low + lax.rem(n, inner_side)
        out_x = jnp.where(ti == inner_low, -WIDTH, WIDTH)
        out_y = jnp.where(tj == inner_low, -WIDTH, WIDTH)
        steps = [(out_x, dy) for dy in range(-WIDTH, WIDTH + 1)]
        steps += [(si - ti, out_y) for si in range(side)]
        pair_sums(ti * side + tj, ti, tj, steps, False)

    edge = own - inner_side * inner_side

    @pl.loop(0, edge)
    def _(n):
        t = jnp.where(n < side, n, jnp.where(n >= edge - side, n + own - edge, 0))
        turn = n - side
        between = (turn // 2 + 1) * side + lax.rem(turn, 2) * (side - 1)
        t = jnp.where((n >= side) & (n < edge - side), between, t)
        steps = [(dx, dy) for dx in range(-WIDTH, WIDTH + 1) for dy in range(-WIDTH, WIDTH + 1)]
        pair_sums(t, t // side, lax.rem(t, side), steps, True)

    in_window = 9 * own
    rows = block_ref[:, 0, :]
    block_lanes = -(-count // 128) * 128
    if block_lanes > count:
        rows = jnp.concatenate(
            [rows, jnp.zeros((block_lanes - count, 128), jnp.float32)], axis=0
        )
    blocks = jnp.concatenate(
        [rows[k * 128 : (k + 1) * 128].T[:MULTI] for k in range(block_lanes // 128)], axis=1
    )
    near_lane = lax.broadcasted_iota(jnp.int32, (MULTI, 128), 1)
    groups = -(-in_window // 128)
    parts = [jnp.zeros((MULTI, 128), jnp.float32) for _ in range(groups)]
    for d in range(9):
        piece = jnp.where(near_lane < own, near_ref[d], 0.0)
        at = d * own
        shift = at % 128
        if shift:
            piece = pltpu.roll(piece, shift, 1)
        parts[at // 128] = parts[at // 128] + piece
    used = in_window % 128
    if used and used + count <= 128:
        first_block = in_window
        parts[-1] = parts[-1] + pltpu.roll(blocks[:, :128], used, 1)
    else:
        first_block = groups * 128
        parts.append(blocks)
    moments = jnp.concatenate(parts, axis=1)
    total_lanes = moments.shape[1]

    lane = lax.broadcasted_iota(jnp.int32, (own, total_lanes), 1)
    row = lax.broadcasted_iota(jnp.int32, (own, total_lanes), 0)
    ti, tj = row // side, row % side
    device = lane // own
    inside = lane % own
    dx = (device // 3 - 1) * side + inside // side - ti
    dy = (device % 3 - 1) * side + inside % side - tj
    reach = jnp.maximum(jnp.abs(dx), jnp.abs(dy))
    weight = jnp.zeros((own, total_lanes), jnp.float32)
    for o, (a, b) in enumerate(CYCLE):
        column = jnp.zeros((own, total_lanes), jnp.float32)
        for t in range(own):
            kept = 1.0 - mask_ref[o, t // side, t % side].astype(jnp.float32)
            column = jnp.where(row == t, kept, column)
        weight = jnp.where((dx == a) & (dy == b), column, weight)
    weight = jnp.where(reach >= 3, 1.0, weight)
    weight = jnp.where(lane < in_window, weight, 0.0)
    number = lane - first_block
    block_x, block_y = number // leaves, number % leaves
    remote = (number >= 0) & (number < count) & (
        jnp.maximum(jnp.abs(block_x - slab), jnp.abs(block_y - leaf)) >= 2
    )
    middle = (side - 1) / 2.0
    far_x = ((block_x - slab) * side - ti).astype(jnp.float32) + middle
    far_y = ((block_y - leaf) * side - tj).astype(jnp.float32) + middle
    weight = jnp.where(remote, 1.0, weight)
    shift_x = jnp.where(remote, far_x, dx.astype(jnp.float32))
    shift_y = jnp.where(remote, far_y, dy.astype(jnp.float32))
    shift_x = jnp.where(weight == 0.0, 1.0, shift_x)
    shift_y = jnp.where(weight == 0.0, 0.0, shift_y)
    denominator = shift_x * shift_x + shift_y * shift_y
    base_x, base_y = shift_x / denominator, -shift_y / denominator
    power_x, power_y = [weight * base_x], [weight * base_y]
    for n in range(1, 2 * ORDER - 1):
        last_x, last_y = power_x[-1] * float(n), power_y[-1] * float(n)
        power_x.append(last_x * base_x - last_y * base_y)
        power_y.append(last_x * base_y + last_y * base_x)
    local_x, local_y = [], []
    moment_x = [
        moments[k : k + 1] * ((-1.0) ** (k + 1) / math.factorial(k)) for k in range(ORDER)
    ]
    moment_y = [
        moments[ORDER + k : ORDER + k + 1] * ((-1.0) ** (k + 1) / math.factorial(k))
        for k in range(ORDER)
    ]
    for m in range(ORDER):
        sum_x = jnp.zeros((own, total_lanes), jnp.float32)
        sum_y = jnp.zeros((own, total_lanes), jnp.float32)
        for k in range(ORDER):
            px, py = power_x[m + k], power_y[m + k]
            sum_x = sum_x + (moment_x[k] * px - moment_y[k] * py)
            sum_y = sum_y + (moment_x[k] * py + moment_y[k] * px)
        scale = 1.0 / math.factorial(m)
        local_x.append(jnp.sum(sum_x, axis=1, keepdims=True) * scale)
        local_y.append(jnp.sum(sum_y, axis=1, keepdims=True) * scale)

    own_x, own_y = own_ref[0], own_ref[1]
    field_x = jnp.broadcast_to(local_x[-1], own_x.shape)
    field_y = jnp.broadcast_to(local_y[-1], own_x.shape)
    for m in range(ORDER - 2, -1, -1):
        field_x, field_y = (
            field_x * own_x - field_y * own_y + local_x[m],
            field_x * own_y + field_y * own_x + local_y[m],
        )
    first = (sum_ref[2] - own_y * sum_ref[0] + field_y) * (1.0 / TWO_PI)
    second = (own_x * sum_ref[0] - sum_ref[1] + field_x) * (1.0 / TWO_PI)
    for i in range(side):
        out_ref[0, i] = first[i * side : (i + 1) * side]
        out_ref[1, i] = second[i * side : (i + 1) * side]


def body(particles, near_mask, *, slabs, leaves):
    side, count = particles.shape[1], particles.shape[3]
    own = side * side
    window = side + 2 * WIDTH
    devices = slabs * leaves
    f32 = jnp.float32
    vmem = pl.BlockSpec(memory_space=pltpu.VMEM)
    smem = pl.BlockSpec(memory_space=pltpu.SMEM)
    strips = [
        pltpu.VMEM((3, span(a, side)[1] * span(b, side)[1], count), f32) for a, b in DIRECTIONS
    ]
    bf16 = jnp.bfloat16
    return pl.pallas_call(
        functools.partial(field_kernel, slabs, leaves, side),
        out_shape=jax.ShapeDtypeStruct((2, side, side, count), f32),
        in_specs=[smem, vmem],
        out_specs=vmem,
        scratch_shapes=[
            pltpu.VMEM((3, window * window, count), f32),
            pltpu.VMEM((3, own, count), f32),
            pltpu.VMEM((9, MULTI, 128), f32),
            pltpu.VMEM((devices, 1, 128), f32),
        ] + strips + strips + [
            pltpu.VMEM((MULTI, 128), f32),
            pltpu.VMEM((1, 128), f32),
            pltpu.SemaphoreType.DMA((8,)), pltpu.SemaphoreType.DMA((8,)),
            pltpu.SemaphoreType.DMA((8,)), pltpu.SemaphoreType.DMA((8,)),
            pltpu.SemaphoreType.DMA((devices,)), pltpu.SemaphoreType.DMA((devices,)),
            pltpu.VMEM((count // 128, FEATURES * (window * window + 8), 128), f32),
            pltpu.VMEM((count // 128, FEATURES * (own + 8), 128), f32),
            pltpu.VMEM((count, FEATURES), bf16),
            pltpu.VMEM((window * window, FEATURES, count), bf16),
            pltpu.VMEM((25, 8, count), f32),
            pltpu.VMEM((3, own, count), f32),
        ],
        compiler_params=pltpu.CompilerParams(
            collective_id=0, has_side_effects=True, vmem_limit_bytes=48 * 1024 * 1024
        ),
        name="field",
    )(near_mask, particles)


def solution(mesh):
    return jax.shard_map(
        functools.partial(body, slabs=mesh.shape["slab"], leaves=mesh.shape["leaf"]),
        mesh=mesh,
        in_specs=(P(None, "slab", "leaf", None), P(None, "slab", "leaf")),
        out_specs=P(None, "slab", "leaf", None),
        check_vma=False,
    )
```
